32 devices in a mesh: roll: 16 (over z, x, core), seq: 2 (over y).
Axes of the slice: x: 2, y: 2, z: 4, core: 2. Of those that a mesh axis runs over, the one named last changes fastest.
Arguments:
- hidden: bfloat16 [16, 1024, 2880], P('roll', 'seq'), may hold values from -6 to 6
- key_value_blocks: bfloat16 [2880, 1024], P('roll'), may hold values from -0.109375 to 0.109375
- block_of: int32 [16], replicated, may hold values from 0 to 15, each once
- queries: bfloat16 [16, 64, 4096], P('roll', 'seq'), may hold values from -480 to 480
- key_pos: int32 [16, 1024], P('roll', 'seq'), may hold values from 0 to 5118, as said below
- query_pos: int32 [16, 64], P('roll', 'seq'), may hold values from 0 to 5118, as said below
Outputs:
- context: bfloat16 [16, 64, 4096], P('roll', 'seq')
The draws below stay inside these ranges and needn't reach their ends.
Inputs may be any that keep to these rules, and one draw needn't show every extreme that they name: Along each sequence key_pos rises by one from that sequence's start; starts lie in 0 to 4095 and some sequence starts at 0, another at 4095. `query_pos`: each query position lies between the first and the last key position of its sequence.
All inputs are finite; a program needn't handle non-finite values.
Results may differ from the reference program's by a relative error of at most 0.017.
The reference program's roundings to bfloat16 on the way count: a program that leaves them out, or rounds other values in their place, can miss the bound.
Values may be sent and summed in bfloat16 or wider, within the bound.
A program may use at most 64 MiB of HBM per device.

```python
import jax
import jax.numpy as jnp
from jax import lax

MODEL_WIDTH = 2880
QUERY_HEAD_COUNT = 64
KEY_VALUE_HEADS = 8
HEAD_WIDTH = 64
CACHED_LENGTH = 1024
QUERY_ROW_COUNT = 64
N_ROLL = 16


def position_helper(key):
    folded = jax.random.fold_in(key, 7)
    key_one, key_two, key_three, key_four = jax.random.split(folded, 4)
    starts = jax.random.randint(key_one, (N_ROLL,), 0, 4096)
    chosen = jax.random.randint(key_three, (), 0, N_ROLL)
    starts = starts.at[chosen].set(4095)
    starts = starts.at[(chosen + 1) % N_ROLL].set(0)
    offsets = jax.random.randint(key_two, (N_ROLL, QUERY_ROW_COUNT), 0, CACHED_LENGTH)
    column = jax.random.randint(key_four, (), 0, QUERY_ROW_COUNT)
    offsets = offsets.at[chosen, column].set(CACHED_LENGTH - 1)
    key_positions = starts[:, None] + jnp.arange(CACHED_LENGTH)[None, :]
    query_positions = starts[:, None] + offsets
    return (key_positions.astype(jnp.int32), query_positions.astype(jnp.int32))


def draw_key_pos(key, part):
    return position_helper(key)[0]


def draw_query_pos(key, part):
    return position_helper(key)[1]


def draw_queries(key, part):
    folded = jax.random.fold_in(key, 11)
    key_one = jax.random.fold_in(folded, 0)
    values = jnp.clip(jax.random.normal(key_one, (N_ROLL, QUERY_ROW_COUNT, QUERY_HEAD_COUNT * HEAD_WIDTH), jnp.float32), -6.0, 6.0)
    return values.astype(jnp.bfloat16)


def block_levels(stream_key, shape, cuts, low, high):
    gain = 1.0
    for dim, shards_of in cuts:
        steps = jax.random.uniform(jax.random.fold_in(jax.random.fold_in(stream_key, 6), dim), (shards_of,), jnp.float32, low / len(cuts), high / len(cuts))
        gain = gain * jnp.repeat(jnp.exp(steps), shape[dim] // shards_of).reshape((-1,) + (1,) * (len(shape) - 1 - dim))
    return gain


def scatter_about(stream_key, dims, spread, most, cuts=(), kind=jnp.bfloat16):
    loudness = block_levels(stream_key, dims, cuts, -0.22, 0.18) if cuts else 1.0
    entries = jax.random.normal(stream_key, dims, jnp.float32) * spread * loudness
    return jnp.minimum(jnp.maximum(entries, -most), most).astype(kind)


def setup_inputs(seed: int = 0) -> dict:
    splits = jax.random.split(jax.random.key(seed), 7)
    hidden = scatter_about(splits[0], (N_ROLL, CACHED_LENGTH, MODEL_WIDTH), 1.0, 6.0, ((0, 16), (1, 2)))
    key_value_blocks = scatter_about(splits[1], (MODEL_WIDTH, 2 * KEY_VALUE_HEADS * HEAD_WIDTH), MODEL_WIDTH ** -0.5, 0.109375, ((0, 16),))
    block_of = jax.random.permutation(splits[2], N_ROLL).astype(jnp.int32)
    queries = draw_queries(jax.random.fold_in(splits[6], 71), 0)
    key_pos = draw_key_pos(jax.random.fold_in(splits[6], 71), 0)
    query_pos = draw_query_pos(jax.random.fold_in(splits[6], 71), 0)
    return dict(hidden=hidden, key_value_blocks=key_value_blocks, block_of=block_of, queries=queries, key_pos=key_pos, query_pos=query_pos)


rope_base = 150000.0

def rotary(vectors, positions):
    head_size = vectors.shape[-1]
    half = head_size // 2
    freq = rope_base ** (-(jnp.arange(half).astype(jnp.float32) * 2.0 / head_size))
    angle = positions.astype(jnp.float32)[:, None] * freq[None, :]
    cosine = jnp.cos(angle)[:, None, :]
    sine = jnp.sin(angle)[:, None, :]
    first = vectors[..., :half]
    second = vectors[..., half:]
    return jnp.concatenate([first * cosine - second * sine, second * cosine + first * sine], axis=-1)

def reference(hidden, key_value_blocks, block_of, queries, key_pos, query_pos):
    block_rows = MODEL_WIDTH // N_ROLL
    column_slice = 2 * KEY_VALUE_HEADS * HEAD_WIDTH
    query_group = QUERY_HEAD_COUNT // KEY_VALUE_HEADS
    stored = key_value_blocks.reshape(N_ROLL, block_rows, column_slice)
    kv_weight = jnp.zeros_like(stored).at[block_of].set(stored).reshape(MODEL_WIDTH, column_slice)

    def one_sequence(index):
        projected_rows = jnp.dot(hidden[index], kv_weight, preferred_element_type=jnp.float32)
        projected_rows = projected_rows.reshape(CACHED_LENGTH, KEY_VALUE_HEADS, 2 * HEAD_WIDTH)
        keys = rotary(projected_rows[..., :HEAD_WIDTH], key_pos[index]).astype(jnp.bfloat16)
        values = projected_rows[..., HEAD_WIDTH:].astype(jnp.bfloat16)
        rotated_rows = rotary(queries[index].astype(jnp.float32).reshape(QUERY_ROW_COUNT, QUERY_HEAD_COUNT, HEAD_WIDTH), query_pos[index])
        rotated_rows = rotated_rows.astype(jnp.bfloat16).reshape(QUERY_ROW_COUNT, KEY_VALUE_HEADS, query_group, HEAD_WIDTH)
        row_pos = jnp.repeat(query_pos[index], query_group)

        def single_head(head):
            query_rows = lax.dynamic_index_in_dim(rotated_rows, head, 1, False).reshape(QUERY_ROW_COUNT * query_group, HEAD_WIDTH)
            head_keys = lax.dynamic_index_in_dim(keys, head, 1, False)
            head_values = lax.dynamic_index_in_dim(values, head, 1, False)
            scores = jnp.dot(query_rows, head_keys.T, preferred_element_type=jnp.float32) * (1.0 / jnp.sqrt(jnp.float32(HEAD_WIDTH)))
            allowed = key_pos[index][None, :] <= row_pos[:, None]
            scores = jnp.where(allowed, scores, -1e+30)
            top = lax.optimization_barrier(jnp.max(scores, axis=1, keepdims=True))
            expo = jnp.where(allowed, jnp.exp(scores - top), 0.0)
            probs = (expo / lax.optimization_barrier(jnp.sum(expo, axis=1, keepdims=True))).astype(jnp.bfloat16)
            return jnp.dot(probs, head_values, preferred_element_type=jnp.float32).astype(jnp.bfloat16)
        head_outputs = lax.map(single_head, jnp.arange(KEY_VALUE_HEADS))
        head_outputs = head_outputs.reshape(KEY_VALUE_HEADS, QUERY_ROW_COUNT, query_group * HEAD_WIDTH).transpose(1, 0, 2)
        return head_outputs.reshape(QUERY_ROW_COUNT, QUERY_HEAD_COUNT * HEAD_WIDTH)
    return lax.map(one_sequence, jnp.arange(N_ROLL))
```

```python
import functools

import jax
import jax.numpy as jnp
import numpy as np
from jax import lax
from jax.experimental import pallas as pl
from jax.experimental.pallas import tpu as pltpu
from jax.sharding import PartitionSpec as P

HEAD_WIDTH = 64
MESH = pl.DeviceIdType.MESH
MASKED = -1e30
rope_base = 150000.0


def kernel(
    n_roll,
    n_seq,
    block_of,
    w_ref,
    hidden_ref,
    q_ref,
    key_pos_ref,
    query_pos_ref,
    freq_col_ref,
    freq_row_ref,
    out_ref,
    w_all,
    hidden_vm,
    h_blocks,
    acc,
    cos_k,
    sin_k,
    kk,
    vv,
    q_all,
    qpos_all,
    o_send,
    o_recv,
    l_send,
    l_recv,
    o_own,
    l_own,
    hidden_sem,
    ring_send,
    ring_recv,
    sib_send,
    sib_recv,
    q_send_sem,
    q_recv_sem,
    qp_send_sem,
    qp_recv_sem,
    o_send_sem,
    o_recv_sem,
    l_send_sem,
    l_recv_sem,
):
    depth, columns = w_ref.shape
    rows = hidden_vm.shape[0]
    q_rows, q_width = q_ref.shape
    heads = columns // (2 * HEAD_WIDTH)
    group = q_width // HEAD_WIDTH // heads
    group_width = group * HEAD_WIDTH
    ring = n_roll // 2
    half_ring = ring // 2
    phases = 2
    width = columns // phases
    heads_per_phase = heads // phases

    me = lax.axis_index("roll")
    seq = lax.axis_index("seq")
    core = me % 2
    chip = me // 2
    along = chip // 2
    side = chip % 2
    place = along * (1 - side) + (ring - 1 - along) * side

    def roll_of(position, which_core):
        position = (position + 2 * ring) % ring
        high = position // half_ring
        where = (1 - high) * (2 * position) + high * (2 * (ring - 1 - position) + 1)
        return 2 * where + which_core

    right = roll_of(place + 1, core)
    left = roll_of(place - 1, core)
    sibling = 2 * chip + 1 - core

    barrier = pltpu.get_barrier_semaphore()
    for other in (left, right, sibling):
        pl.semaphore_signal(barrier, inc=1, device_id=(other, seq), device_id_type=MESH)
    for i in range(1, n_seq):
        pl.semaphore_signal(
            barrier, inc=1, device_id=(me, (seq + i) % n_seq), device_id_type=MESH
        )
    pl.semaphore_wait(barrier, 3 + n_seq - 1)

    hidden_copy = pltpu.make_async_copy(hidden_ref, hidden_vm, hidden_sem)
    hidden_copy.start()

    def cols(phase, part):
        if part is None:
            return pl.ds(phase * width, width)
        return pl.ds(phase * width + part * (width // 2), width // 2)

    def ring_copy(phase, direction, step, part, own=False):
        origin = roll_of(place - (step - 1) * (1 - 2 * direction), core)
        c = cols(phase, part)
        return pltpu.make_async_remote_copy(
            src_ref=w_ref.at[:, c] if own else w_all.at[origin, :, c],
            dst_ref=w_all.at[origin, :, c],
            send_sem=ring_send.at[phase, direction, step - 1],
            recv_sem=ring_recv.at[phase, direction, step - 1],
            device_id=(right if direction == 0 else left, seq),
            device_id_type=MESH,
        )

    def ring_arrival(phase, direction, step, part):
        origin = roll_of(place - step * (1 - 2 * direction), core)
        c = cols(phase, part)
        return pltpu.make_async_remote_copy(
            src_ref=w_all.at[origin, :, c],
            dst_ref=w_all.at[origin, :, c],
            send_sem=ring_send.at[phase, direction, step - 1],
            recv_sem=ring_recv.at[phase, direction, step - 1],
            device_id=(right if direction == 0 else left, seq),
            device_id_type=MESH,
        )

    def sib_copy(phase, direction, step, part, which_core, own=False):
        origin = roll_of(place - step * (1 - 2 * direction), which_core)
        c = cols(phase, part)
        return pltpu.make_async_remote_copy(
            src_ref=w_ref.at[:, c] if own else w_all.at[origin, :, c],
            dst_ref=w_all.at[origin, :, c],
            send_sem=sib_send.at[phase, direction, step],
            recv_sem=sib_recv.at[phase, direction, step],
            device_id=(sibling, seq),
            device_id_type=MESH,
        )

    def start_phase(phase):
        for direction in range(2):
            ring_copy(phase, direction, 1, None if half_ring > 1 else direction, own=True).start()
        sib_copy(phase, 0, 0, None, core, own=True).start()

    start_phase(0)

    lane = lax.broadcasted_iota(jnp.int32, (q_rows, 128), 1)
    on_diag = lax.broadcasted_iota(jnp.int32, (q_rows, q_rows), 0) == lax.broadcasted_iota(
        jnp.int32, (q_rows, q_rows), 1
    )
    q_pos_row = query_pos_ref[...].astype(jnp.float32)
    q_pos_col = jnp.sum(
        jnp.where(on_diag, jnp.broadcast_to(q_pos_row, (q_rows, q_rows)), 0.0),
        axis=1,
        keepdims=True,
    )
    qpos_all[seq] = jnp.broadcast_to(q_pos_col, (q_rows, 128))
    q_angle = q_pos_col * freq_row_ref[...]
    q_cos = jnp.cos(q_angle)
    q_sin = jnp.sin(q_angle)
    first_half = lane % HEAD_WIDTH < HEAD_WIDTH // 2
    q_sin = jnp.where(first_half, -q_sin, q_sin)
    scale = HEAD_WIDTH ** -0.5
    for t in range(q_width // 128):
        x = q_ref[:, t * 128 : (t + 1) * 128].astype(jnp.float32)
        swapped = jnp.where(
            first_half,
            pltpu.roll(x, 128 - HEAD_WIDTH // 2, 1),
            pltpu.roll(x, HEAD_WIDTH // 2, 1),
        )
        rotated = (x * q_cos + swapped * q_sin).astype(jnp.bfloat16)
        q_all[seq, :, t * 128 : (t + 1) * 128] = (
            rotated.astype(jnp.float32) * scale
        ).astype(jnp.bfloat16)

    def q_copies(i, origin):
        target = (me, (seq + i) % n_seq)
        return (
            pltpu.make_async_remote_copy(
                src_ref=q_all.at[origin],
                dst_ref=q_all.at[origin],
                send_sem=q_send_sem.at[i],
                recv_sem=q_recv_sem.at[i],
                device_id=target,
                device_id_type=MESH,
            ),
            pltpu.make_async_remote_copy(
                src_ref=qpos_all.at[origin],
                dst_ref=qpos_all.at[origin],
                send_sem=qp_send_sem.at[i],
                recv_sem=qp_recv_sem.at[i],
                device_id=target,
                device_id_type=MESH,
            ),
        )

    for i in range(1, n_seq):
        for copy in q_copies(i, seq):
            copy.start()

    k_pos = key_pos_ref[...].astype(jnp.float32)
    k_angle = freq_col_ref[...] * k_pos
    cos_k[...] = jnp.cos(k_angle)
    sin_k[...] = jnp.sin(k_angle)

    hidden_copy.wait()
    for b in range(n_roll):
        h_blocks[b] = hidden_vm[:, b * depth : (b + 1) * depth]

    def multiply(block, phase, own=False, first=False):
        logical = block_of[block]
        c = cols(phase, None)
        weights = w_ref[:, c] if own else w_all[block, :, c]
        product = jnp.dot(h_blocks[logical], weights, preferred_element_type=jnp.float32)
        if first:
            acc[:, c] = product
        else:
            acc[:, c] += product

    for phase in range(phases):
        multiply(me, phase, own=True, first=True)

        def step_body(step, carry):
            for direction in range(2):
                ring_arrival(phase, direction, step, None).wait_recv()

                if half_ring > 2:

                    @pl.when(step < half_ring - 1)
                    def _():
                        ring_copy(phase, direction, step + 1, None).start()

                @pl.when(step == half_ring - 1)
                def _():
                    ring_copy(phase, direction, step + 1, direction).start()

                sib_copy(phase, direction, step, None, core).start()
            multiply(roll_of(place - step, core), phase)
            multiply(roll_of(place + step, core), phase)

            @pl.when(step == 1)
            def _():
                sib_copy(phase, 0, 0, None, 1 - core).wait_recv()
                multiply(sibling, phase)

            @pl.when(step > 1)
            def _():
                for direction in range(2):
                    sib_copy(phase, direction, step - 1, None, 1 - core).wait_recv()
                    multiply(
                        roll_of(place - (step - 1) * (1 - 2 * direction), 1 - core), phase
                    )

            return carry

        lax.fori_loop(1, half_ring, step_body, 0)
        if phase + 1 < phases:
            start_phase(phase + 1)
        for direction in range(2):
            ring_arrival(phase, direction, half_ring, direction).wait_recv()
            sib_copy(phase, direction, half_ring, direction, core).start()
        for direction in range(2):
            sib_copy(phase, direction, half_ring - 1, None, 1 - core).wait_recv()
            multiply(
                roll_of(place - (half_ring - 1) * (1 - 2 * direction), 1 - core), phase
            )
        multiply(roll_of(place + half_ring, core), phase)
        for direction in range(2):
            sib_copy(phase, direction, half_ring, direction, 1 - core).wait_recv()
        multiply(roll_of(place + half_ring, 1 - core), phase)

    lane_k = lax.broadcasted_iota(jnp.int32, (rows, 128), 1)
    cos_keys = cos_k[...]
    sin_keys = sin_k[...]

    def prepare(h, carry):
        both = acc[:, pl.ds(pl.multiple_of(h * 128, 128), 128)]
        turned = both.T
        first = turned[: HEAD_WIDTH // 2]
        second = turned[HEAD_WIDTH // 2 : HEAD_WIDTH]
        key = jnp.concatenate(
            [first * cos_keys - second * sin_keys, second * cos_keys + first * sin_keys], axis=0
        )
        kk[h] = jnp.concatenate([key, key], axis=0).astype(jnp.bfloat16)
        value = jnp.where(lane_k < HEAD_WIDTH, pltpu.roll(both, HEAD_WIDTH, 1), both)
        vv[h] = jnp.concatenate([value, jnp.ones_like(value)], axis=1).astype(jnp.bfloat16)
        return carry

    lax.fori_loop(0, heads, prepare, 0)

    def o_copy(i, h):
        c = pl.ds(pl.multiple_of(h * group_width, group_width), group_width)
        return pltpu.make_async_remote_copy(
            src_ref=o_send.at[i, :, c],
            dst_ref=o_recv.at[i, :, c],
            send_sem=o_send_sem.at[i, h],
            recv_sem=o_recv_sem.at[i, h],
            device_id=(me, (seq + i) % n_seq),
            device_id_type=MESH,
        )

    def l_copy(i):
        return pltpu.make_async_remote_copy(
            src_ref=l_send.at[i],
            dst_ref=l_recv.at[i],
            send_sem=l_send_sem.at[i],
            recv_sem=l_recv_sem.at[i],
            device_id=(me, (seq + i) % n_seq),
            device_id_type=MESH,
        )

    left_lanes = lane < HEAD_WIDTH
    pairs = group // 2

    def attend(i, h, allowed, packed):
        target = (seq + i) % n_seq
        base = pl.multiple_of(h * group_width, group_width)
        queries = q_all[target, :, pl.ds(base, group_width)]
        parts = []
        for j in range(pairs):
            two = queries[:, j * 128 : (j + 1) * 128]
            parts.append(jnp.where(left_lanes, two, jnp.zeros_like(two)))
            parts.append(jnp.where(left_lanes, jnp.zeros_like(two), two))
        stacked = jnp.concatenate(parts, axis=0)
        scores = jnp.dot(stacked, kk[h], preferred_element_type=jnp.float32)
        scores = scores.reshape(group, q_rows, rows)
        scores = jnp.where(allowed[None], scores, MASKED).reshape(group * q_rows, rows)
        top = jnp.max(scores, axis=1, keepdims=True)
        probs = jnp.exp(scores - top).astype(jnp.bfloat16)
        result = jnp.dot(probs, vv[h], preferred_element_type=jnp.float32)
        total = result[:, 128:]
        normal = result[:, :128] / total
        logs = top + jnp.log(total)
        for j in range(pairs):
            even = slice(2 * j * q_rows, (2 * j + 1) * q_rows)
            odd = slice((2 * j + 1) * q_rows, (2 * j + 2) * q_rows)
            tile = jnp.where(left_lanes, normal[even], normal[odd])
            c = pl.ds(pl.multiple_of(base + j * 128, 128), 128)
            if i == 0:
                o_own[:, c] = tile
            else:
                o_send[i, :, c] = tile.astype(jnp.bfloat16)
            packed = jnp.where(lane == h * group + 2 * j, logs[even], packed)
            packed = jnp.where(lane == h * group + 2 * j + 1, logs[odd], packed)
        return packed

    for i in list(range(1, n_seq)) + [0]:
        if i:
            for copy in q_copies(i, (seq - i + n_seq) % n_seq):
                copy.wait_recv()

    for i in list(range(1, n_seq)) + [0]:
        target = (seq + i) % n_seq
        allowed = k_pos <= qpos_all[target][:, 0:1]

        def one_head(h, packed):
            packed = attend(i, h, allowed, packed)
            if i:
                o_copy(i, h).start()
            return packed

        packed = lax.fori_loop(0, heads, one_head, jnp.zeros((q_rows, 128), jnp.float32))
        if i:
            l_send[i] = packed
            l_copy(i).start()
        else:
            l_own[...] = packed

    for i in range(1, n_seq):
        l_copy(i).wait_recv()

        def wait_head(h, carry):
            o_copy(i, h).wait_recv()
            return carry

        lax.fori_loop(0, heads, wait_head, 0)

    logs = [l_own[...]] + [l_recv[i] for i in range(1, n_seq)]
    top = functools.reduce(jnp.maximum, logs)
    shares = [jnp.exp(entry - top) for entry in logs]
    whole = functools.reduce(jnp.add, shares)
    shares = [entry / whole for entry in shares]
    for t in range(q_width // 128):
        c = slice(t * 128, (t + 1) * 128)
        total = None
        for i in range(n_seq):
            share = jnp.where(
                left_lanes, shares[i][:, 2 * t : 2 * t + 1], shares[i][:, 2 * t + 1 : 2 * t + 2]
            )
            part = o_own[:, c] if i == 0 else o_recv[i, :, c].astype(jnp.float32)
            total = share * part if total is None else total + share * part
        out_ref[:, c] = total.astype(jnp.bfloat16)

    for i in range(1, n_seq):
        for copy in q_copies(i, seq):
            copy.wait_send()
        l_copy(i).wait_send()

        def sent_head(h, carry):
            o_copy(i, h).wait_send()
            return carry

        lax.fori_loop(0, heads, sent_head, 0)
    for phase in range(phases):
        sib_copy(phase, 0, 0, None, core, own=True).wait_send()

        def sent_step(step, carry):
            for direction in range(2):
                ring_copy(phase, direction, step, None).wait_send()
                sib_copy(phase, direction, step, None, core).wait_send()
            return carry

        lax.fori_loop(1, half_ring, sent_step, 0)
        for direction in range(2):
            ring_copy(phase, direction, half_ring, direction).wait_send()
            sib_copy(phase, direction, half_ring, direction, core).wait_send()


def shards(n_roll, n_seq, hidden, key_value_blocks, block_of, queries, key_pos, query_pos):
    rows, model_width = hidden.shape[1:]
    depth, columns = key_value_blocks.shape
    q_rows, q_width = queries.shape[1:]
    heads = columns // (2 * HEAD_WIDTH)
    half = HEAD_WIDTH // 2
    freq = rope_base ** (-(np.arange(half) * 2.0 / HEAD_WIDTH))
    freq = freq.astype(np.float32)
    vmem = pl.BlockSpec(memory_space=pltpu.VMEM)
    half_ring = n_roll // 4
    bf16, f32 = jnp.bfloat16, jnp.float32
    dma = pltpu.SemaphoreType.DMA
    out = pl.pallas_call(
        functools.partial(kernel, n_roll, n_seq),
        out_shape=jax.ShapeDtypeStruct((q_rows, q_width), bf16),
        in_specs=[
            pl.BlockSpec(memory_space=pltpu.SMEM),
            vmem,
            pl.BlockSpec(memory_space=pl.ANY),
            vmem,
            vmem,
            vmem,
            vmem,
            vmem,
        ],
        out_specs=vmem,
        scratch_shapes=[
            pltpu.VMEM((n_roll, depth, columns), bf16),
            pltpu.VMEM((rows, model_width), bf16),
            pltpu.VMEM((n_roll, rows, depth), bf16),
            pltpu.VMEM((rows, columns), f32),
            pltpu.VMEM((half, rows), f32),
            pltpu.VMEM((half, rows), f32),
            pltpu.VMEM((heads, 128, rows), bf16),
            pltpu.VMEM((heads, rows, 256), bf16),
            pltpu.VMEM((n_seq, q_rows, q_width), bf16),
            pltpu.VMEM((n_seq, q_rows, 128), f32),
            pltpu.VMEM((n_seq, q_rows, q_width), bf16),
            pltpu.VMEM((n_seq, q_rows, q_width), bf16),
            pltpu.VMEM((n_seq, q_rows, 128), f32),
            pltpu.VMEM((n_seq, q_rows, 128), f32),
            pltpu.VMEM((q_rows, q_width), f32),
            pltpu.VMEM((q_rows, 128), f32),
            dma,
            dma((2, 2, half_ring)),
            dma((2, 2, half_ring)),
            dma((2, 2, half_ring + 1)),
            dma((2, 2, half_ring + 1)),
            dma((n_seq,)),
            dma((n_seq,)),
            dma((n_seq,)),
            dma((n_seq,)),
            dma((n_seq, heads)),
            dma((n_seq, heads)),
            dma((n_seq,)),
            dma((n_seq,)),
        ],
        compiler_params=pltpu.CompilerParams(
            collective_id=0, has_side_effects=True, vmem_limit_bytes=52 * 1024 * 1024
        ),
        cost_estimate=pl.CostEstimate(
            flops=2 * rows * model_width * columns,
            bytes_accessed=2 * rows * model_width,
            transcendentals=0,
        ),
    )(
        block_of,
        key_value_blocks,
        hidden[0],
        queries[0],
        key_pos,
        query_pos,
        jnp.asarray(freq[:, None]),
        jnp.asarray(np.tile(freq, 128 // half)[None]),
    )
    return out[None]


def solution(mesh):
    return jax.shard_map(
        functools.partial(shards, mesh.shape["roll"], mesh.shape["seq"]),
        mesh=mesh,
        in_specs=(
            P("roll", "seq", None),
            P("roll", None),
            P(),
            P("roll", "seq", None),
            P("roll", "seq"),
            P("roll", "seq"),
        ),
        out_specs=P("roll", "seq", None),
        check_vma=False,
    )
```

```python
import functools

import jax
import jax.numpy as jnp
import numpy as np
from jax import lax
from jax.experimental import pallas as pl
from jax.experimental.pallas import tpu as pltpu
from jax.sharding import PartitionSpec as P

HEAD_WIDTH = 64
MESH = pl.DeviceIdType.MESH
MASKED = -1e30
rope_base = 150000.0


def kernel(
    n_roll,
    n_seq,
    block_of,
    w_ref,
    hidden_ref,
    q_ref,
    key_pos_ref,
    query_pos_ref,
    freq_col_ref,
    freq_row_ref,
    out_ref,
    w_all,
    hidden_vm,
    h_blocks,
    acc,
    cos_k,
    sin_k,
    q_all,
    qpos_all,
    o_send,
    o_recv,
    l_send,
    l_recv,
    o_own,
    hidden_sem,
    ring_send,
    ring_recv,
    sib_send,
    sib_recv,
    own_send,
    own_recv,
    q_send_sem,
    q_recv_sem,
    qp_send_sem,
    qp_recv_sem,
    o_send_sem,
    o_recv_sem,
    l_send_sem,
    l_recv_sem,
):
    depth, columns = w_ref.shape
    rows = hidden_vm.shape[1]
    q_rows, q_width = q_ref.shape
    heads = columns // (2 * HEAD_WIDTH)
    group = q_width // HEAD_WIDTH // heads
    group_width = group * HEAD_WIDTH
    ring = n_roll // 2
    half_ring = ring // 2
    phase_heads = 2
    phases = heads // phase_heads
    width = columns // phases

    me = lax.axis_index("roll")
    seq = lax.axis_index("seq")
    core = me % 2
    chip = me // 2
    along = chip // 2
    side = chip % 2
    place = along * (1 - side) + (ring - 1 - along) * side

    def roll_of(position, which_core):
        position = (position + 2 * ring) % ring
        high = position // half_ring
        where = (1 - high) * (2 * position) + high * (2 * (ring - 1 - position) + 1)
        return 2 * where + which_core

    right = roll_of(place + 1, core)
    left = roll_of(place - 1, core)
    sibling = 2 * chip + 1 - core

    barrier = pltpu.get_barrier_semaphore()
    for other in (left, right, sibling):
        pl.semaphore_signal(barrier, inc=1, device_id=(other, seq), device_id_type=MESH)
    for i in range(1, n_seq):
        pl.semaphore_signal(
            barrier, inc=1, device_id=(me, (seq + i) % n_seq), device_id_type=MESH
        )
    pl.semaphore_wait(barrier, 3 + n_seq - 1)

    hidden_copy = pltpu.make_async_copy(hidden_ref, hidden_vm, hidden_sem)
    hidden_copy.start()

    def cols(phase):
        return pl.ds(phase * width, width)

    def some_heads(phase, part):
        if part is None:
            return pl.ds(phase * phase_heads, phase_heads)
        return pl.ds(phase * phase_heads + part, 1)

    def origin_of(direction, step, which_core):
        return roll_of(place - step * (1 - 2 * direction), which_core)

    def ring_copy(phase, direction, step, part, arrival=False):
        origin = origin_of(direction, step if arrival else step - 1, core)
        block = w_all.at[origin, some_heads(phase, part)]
        return pltpu.make_async_remote_copy(
            src_ref=block,
            dst_ref=block,
            send_sem=ring_send.at[phase, direction, step - 1],
            recv_sem=ring_recv.at[phase, direction, step - 1],
            device_id=(right if direction == 0 else left, seq),
            device_id_type=MESH,
        )

    def ring_arrival(phase, direction, step, part):
        return ring_copy(phase, direction, step, part, arrival=True)

    def sib_copy(phase, direction, step, part, which_core):
        block = w_all.at[origin_of(direction, step, which_core), some_heads(phase, part)]
        return pltpu.make_async_remote_copy(
            src_ref=block,
            dst_ref=block,
            send_sem=sib_send.at[phase, direction, step - 1],
            recv_sem=sib_recv.at[phase, direction, step - 1],
            device_id=(sibling, seq),
            device_id_type=MESH,
        )

    def sib_own(origin):
        return pltpu.make_async_remote_copy(
            src_ref=w_all.at[origin],
            dst_ref=w_all.at[origin],
            send_sem=own_send,
            recv_sem=own_recv,
            device_id=(sibling, seq),
            device_id_type=MESH,
        )

    for h in range(heads):
        w_all[me, h] = w_ref[:, h * 128 : (h + 1) * 128]

    def start_phase(phase):
        for direction in range(2):
            ring_copy(phase, direction, 1, None).start()

    start_phase(0)
    sib_own(me).start()
    start_phase(1)

    lane = lax.broadcasted_iota(jnp.int32, (q_rows, 128), 1)
    on_diag = lax.broadcasted_iota(jnp.int32, (q_rows, q_rows), 0) == lax.broadcasted_iota(
        jnp.int32, (q_rows, q_rows), 1
    )
    q_pos_row = query_pos_ref[...].astype(jnp.float32)
    q_pos_col = jnp.sum(
        jnp.where(on_diag, jnp.broadcast_to(q_pos_row, (q_rows, q_rows)), 0.0),
        axis=1,
        keepdims=True,
    )
    qpos_all[seq] = jnp.broadcast_to(q_pos_col, (q_rows, 128))
    q_angle = q_pos_col * freq_row_ref[...]
    q_cos = jnp.cos(q_angle)
    q_sin = jnp.sin(q_angle)
    first_half = lane % HEAD_WIDTH < HEAD_WIDTH // 2
    q_sin = jnp.where(first_half, -q_sin, q_sin)
    scale = HEAD_WIDTH ** -0.5
    for t in range(q_width // 128):
        x = q_ref[:, t * 128 : (t + 1) * 128].astype(jnp.float32)
        swapped = jnp.where(
            first_half,
            pltpu.roll(x, 128 - HEAD_WIDTH // 2, 1),
            pltpu.roll(x, HEAD_WIDTH // 2, 1),
        )
        rotated = (x * q_cos + swapped * q_sin).astype(jnp.bfloat16)
        q_all[seq, :, t * 128 : (t + 1) * 128] = (
            rotated.astype(jnp.float32) * scale
        ).astype(jnp.bfloat16)

    def q_copies(i, origin):
        target = (me, (seq + i) % n_seq)
        return (
            pltpu.make_async_remote_copy(
                src_ref=q_all.at[origin],
                dst_ref=q_all.at[origin],
                send_sem=q_send_sem.at[i],
                recv_sem=q_recv_sem.at[i],
                device_id=target,
                device_id_type=MESH,
            ),
            pltpu.make_async_remote_copy(
                src_ref=qpos_all.at[origin],
                dst_ref=qpos_all.at[origin],
                send_sem=qp_send_sem.at[i],
                recv_sem=qp_recv_sem.at[i],
                device_id=target,
                device_id_type=MESH,
            ),
        )

    for i in range(1, n_seq):
        for copy in q_copies(i, seq):
            copy.start()

    k_pos = key_pos_ref[...].astype(jnp.float32)
    k_angle = freq_col_ref[...] * k_pos
    cos_k[...] = jnp.cos(k_angle)
    sin_k[...] = jnp.sin(k_angle)

    hidden_copy.wait()
    for b in range(n_roll):
        h_blocks[b] = hidden_vm[b * depth : (b + 1) * depth, :].T

    def product(block, phase):
        weights = jnp.concatenate(
            [w_all[block, phase * phase_heads + j] for j in range(phase_heads)], axis=1
        )
        return jnp.dot(h_blocks[block_of[block]], weights, preferred_element_type=jnp.float32)

    def multiply(block, phase):
        acc[:, cols(phase)] += product(block, phase)

    def o_copy(i, h):
        c = pl.ds(pl.multiple_of(h * group_width, group_width), group_width)
        return pltpu.make_async_remote_copy(
            src_ref=o_send.at[i, :, c],
            dst_ref=o_recv.at[i, :, c],
            send_sem=o_send_sem.at[i, h],
            recv_sem=o_recv_sem.at[i, h],
            device_id=(me, (seq + i) % n_seq),
            device_id_type=MESH,
        )

    def l_copy(i):
        return pltpu.make_async_remote_copy(
            src_ref=l_send.at[i],
            dst_ref=l_recv.at[i],
            send_sem=l_send_sem.at[i],
            recv_sem=l_recv_sem.at[i],
            device_id=(me, (seq + i) % n_seq),
            device_id_type=MESH,
        )

    left_lanes = lane < HEAD_WIDTH
    pairs = group // 2

    def attend(i, h, keys, values):
        target = (seq + i) % n_seq
        base = h * group_width
        queries = q_all[target, :, pl.ds(pl.multiple_of(base, group_width), group_width)]
        parts = []
        for j in range(pairs):
            two = queries[:, j * 128 : (j + 1) * 128]
            parts.append(jnp.where(left_lanes, two, jnp.zeros_like(two)))
            parts.append(jnp.where(left_lanes, jnp.zeros_like(two), two))
        stacked = jnp.concatenate(parts, axis=0)
        allowed = k_pos <= qpos_all[target][:, 0:1]
        scores = jnp.dot(stacked, keys, preferred_element_type=jnp.float32)
        scores = scores.reshape(group, q_rows, rows)
        scores = jnp.where(allowed[None], scores, MASKED).reshape(group * q_rows, rows)
        top = jnp.max(scores, axis=1, keepdims=True)
        probs = jnp.exp(scores - top).astype(jnp.bfloat16)
        result = jnp.dot(probs, values, preferred_element_type=jnp.float32)
        total = result[:, 128:]
        normal = result[:, :128] / total
        logs = top + jnp.log(total)
        packed = l_send[i]
        for j in range(pairs):
            even = slice(2 * j * q_rows, (2 * j + 1) * q_rows)
            odd = slice((2 * j + 1) * q_rows, (2 * j + 2) * q_rows)
            tile = jnp.where(left_lanes, normal[even], normal[odd])
            c = pl.ds(pl.multiple_of(base + j * 128, 128), 128)
            if i == 0:
                o_own[:, c] = tile
            else:
                o_send[i, :, c] = tile.astype(jnp.bfloat16)
            packed = jnp.where(lane == h * group + 2 * j, logs[even], packed)
            packed = jnp.where(lane == h * group + 2 * j + 1, logs[odd], packed)
        l_send[i] = packed

    l_send[...] = jnp.zeros_like(l_send)
    lane_k = lax.broadcasted_iota(jnp.int32, (rows, 128), 1)

    def one_head(h):
        both = acc[:, pl.ds(pl.multiple_of(h * 128, 128), 128)]
        turned = both.T
        first = turned[: HEAD_WIDTH // 2]
        second = turned[HEAD_WIDTH // 2 : HEAD_WIDTH]
        cos_keys = cos_k[...]
        sin_keys = sin_k[...]
        key = jnp.concatenate(
            [first * cos_keys - second * sin_keys, second * cos_keys + first * sin_keys], axis=0
        )
        keys = jnp.concatenate([key, key], axis=0).astype(jnp.bfloat16)
        value = jnp.where(lane_k < HEAD_WIDTH, pltpu.roll(both, HEAD_WIDTH, 1), both)
        values = jnp.concatenate([value, jnp.ones_like(value)], axis=1).astype(jnp.bfloat16)
        for i in list(range(1, n_seq)) + [0]:
            attend(i, h, keys, values)
        for i in range(1, n_seq):
            o_copy(i, h).start()

    in_loop = min(phase_heads, half_ring - 1)
    for phase in range(phases):
        acc[:, cols(phase)] = product(me, phase)

        def step_body(step, carry):
            for direction in range(2):
                ring_arrival(phase, direction, step, None).wait_recv()

                @pl.when(step < half_ring - 1)
                def _():
                    ring_copy(phase, direction, step + 1, None).start()

                @pl.when(step == half_ring - 1)
                def _():
                    ring_copy(phase, direction, step + 1, direction).start()

                sib_copy(phase, direction, step, None, core).start()
            multiply(origin_of(0, step, core), phase)
            multiply(origin_of(1, step, core), phase)

            @pl.when(step > 1)
            def _():
                for direction in range(2):
                    sib_copy(phase, direction, step - 1, None, 1 - core).wait_recv()
                    multiply(origin_of(direction, step - 1, 1 - core), phase)

            if phase > 0:

                @pl.when(step <= in_loop)
                def _():
                    one_head((phase - 1) * phase_heads + step - 1)

            return carry

        lax.fori_loop(1, half_ring, step_body, 0)
        if phase + 2 < phases:
            start_phase(phase + 2)
        if phase == 0:
            sib_own(sibling).wait_recv()
            for i in range(1, n_seq):
                for copy in q_copies(i, (seq - i + n_seq) % n_seq):
                    copy.wait_recv()
        multiply(sibling, phase)
        for direction in range(2):
            sib_copy(phase, direction, half_ring - 1, None, 1 - core).wait_recv()
            multiply(origin_of(direction, half_ring - 1, 1 - core), phase)
        for direction in range(2):
            ring_arrival(phase, direction, half_ring, direction).wait_recv()
            sib_copy(phase, direction, half_ring, direction, core).start()
        multiply(origin_of(0, half_ring, core), phase)
        if phase > 0:
            for left_over in range(in_loop, phase_heads):
                one_head((phase - 1) * phase_heads + left_over)
        for direction in range(2):
            sib_copy(phase, direction, half_ring, direction, 1 - core).wait_recv()
        multiply(origin_of(0, half_ring, 1 - core), phase)

    for j in range(phase_heads):
        one_head((phases - 1) * phase_heads + j)
    for i in range(1, n_seq):
        l_copy(i).start()

    for i in range(1, n_seq):
        l_copy(i).wait_recv()

        def wait_head(h, carry):
            o_copy(i, h).wait_recv()
            return carry

        lax.fori_loop(0, heads, wait_head, 0)

    logs = [l_send[0]] + [l_recv[i] for i in range(1, n_seq)]
    top = functools.reduce(jnp.maximum, logs)
    shares = [jnp.exp(entry - top) for entry in logs]
    whole = functools.reduce(jnp.add, shares)
    shares = [entry / whole for entry in shares]
    for t in range(q_width // 128):
        c = slice(t * 128, (t + 1) * 128)
        total = None
        for i in range(n_seq):
            share = jnp.where(
                left_lanes, shares[i][:, 2 * t : 2 * t + 1], shares[i][:, 2 * t + 1 : 2 * t + 2]
            )
            part = o_own[:, c] if i == 0 else o_recv[i, :, c].astype(jnp.float32)
            total = share * part if total is None else total + share * part
        out_ref[:, c] = total.astype(jnp.bfloat16)

    for i in range(1, n_seq):
        for copy in q_copies(i, seq):
            copy.wait_send()
        l_copy(i).wait_send()

        def sent_head(h, carry):
            o_copy(i, h).wait_send()
            return carry

        lax.fori_loop(0, heads, sent_head, 0)
    sib_own(me).wait_send()
    for phase in range(phases):

        def sent_step(step, carry):
            for direction in range(2):
                ring_copy(phase, direction, step, None).wait_send()
                sib_copy(phase, direction, step, None, core).wait_send()
            return carry

        lax.fori_loop(1, half_ring, sent_step, 0)
        for direction in range(2):
            ring_copy(phase, direction, half_ring, direction).wait_send()
            sib_copy(phase, direction, half_ring, direction, core).wait_send()


def shards(n_roll, n_seq, hidden, key_value_blocks, block_of, queries, key_pos, query_pos):
    rows, model_width = hidden.shape[1:]
    depth, columns = key_value_blocks.shape
    q_rows, q_width = queries.shape[1:]
    heads = columns // (2 * HEAD_WIDTH)
    half = HEAD_WIDTH // 2
    freq = rope_base ** (-(np.arange(half) * 2.0 / HEAD_WIDTH))
    freq = freq.astype(np.float32)
    vmem = pl.BlockSpec(memory_space=pltpu.VMEM)
    half_ring = n_roll // 4
    phases = heads // 2
    bf16, f32 = jnp.bfloat16, jnp.float32
    dma = pltpu.SemaphoreType.DMA
    out = pl.pallas_call(
        functools.partial(kernel, n_roll, n_seq),
        out_shape=jax.ShapeDtypeStruct((q_rows, q_width), bf16),
        in_specs=[
            pl.BlockSpec(memory_space=pltpu.SMEM),
            vmem,
            pl.BlockSpec(memory_space=pl.ANY),
            vmem,
            vmem,
            vmem,
            vmem,
            vmem,
        ],
        out_specs=vmem,
        scratch_shapes=[
            pltpu.VMEM((n_roll, heads, depth, 128), bf16),
            pltpu.VMEM((model_width, rows), bf16),
            pltpu.VMEM((n_roll, rows, depth), bf16),
            pltpu.VMEM((rows, columns), f32),
            pltpu.VMEM((half, rows), f32),
            pltpu.VMEM((half, rows), f32),
            pltpu.VMEM((n_seq, q_rows, q_width), bf16),
            pltpu.VMEM((n_seq, q_rows, 128), f32),
            pltpu.VMEM((n_seq, q_rows, q_width), bf16),
            pltpu.VMEM((n_seq, q_rows, q_width), bf16),
            pltpu.VMEM((n_seq, q_rows, 128), f32),
            pltpu.VMEM((n_seq, q_rows, 128), f32),
            pltpu.VMEM((q_rows, q_width), f32),
            dma,
            dma((phases, 2, half_ring)),
            dma((phases, 2, half_ring)),
            dma((phases, 2, half_ring)),
            dma((phases, 2, half_ring)),
            dma,
            dma,
            dma((n_seq,)),
            dma((n_seq,)),
            dma((n_seq,)),
            dma((n_seq,)),
            dma((n_seq, heads)),
            dma((n_seq, heads)),
            dma((n_seq,)),
            dma((n_seq,)),
        ],
        compiler_params=pltpu.CompilerParams(
            collective_id=0, has_side_effects=True, vmem_limit_bytes=52 * 1024 * 1024
        ),
        cost_estimate=pl.CostEstimate(
            flops=2 * rows * model_width * columns,
            bytes_accessed=2 * rows * model_width,
            transcendentals=0,
        ),
    )(
        block_of,
        key_value_blocks,
        hidden[0].T,
        queries[0],
        key_pos,
        query_pos,
        jnp.asarray(freq[:, None]),
        jnp.asarray(np.tile(freq, 128 // half)[None]),
    )
    return out[None]


def solution(mesh):
    return jax.shard_map(
        functools.partial(shards, mesh.shape["roll"], mesh.shape["seq"]),
        mesh=mesh,
        in_specs=(
            P("roll", "seq", None),
            P("roll", None),
            P(),
            P("roll", "seq", None),
            P("roll", "seq"),
            P("roll", "seq"),
        ),
        out_specs=P("roll", "seq", None),
        check_vma=False,
    )
```

```python
import functools
import math

import jax
import jax.numpy as jnp
import numpy as np
from jax import lax
from jax.experimental import pallas as pl
from jax.experimental.pallas import tpu as pltpu
from jax.sharding import PartitionSpec as P

HEAD_WIDTH = 64
MESH = pl.DeviceIdType.MESH
MASKED = -1e30
rope_base = 150000.0


def phase_plan(heads):
    return ((0, heads // 2), (heads // 2, heads // 4), (heads // 2 + heads // 4, heads // 4))


def kernel(
    n_roll,
    n_seq,
    block_of,
    w_ref,
    hidden_ref,
    q_hbm,
    key_pos_hbm,
    query_pos_hbm,
    freq_hbm,
    out_ref,
    q_ref,
    key_pos_ref,
    query_pos_ref,
    freq_ref,
    w_all,
    hidden_vm,
    h_blocks,
    h_all,
    w_phase,
    acc,
    cos_k,
    sin_k,
    q_all,
    qpos_all,
    o_send,
    o_recv,
    l_send,
    l_recv,
    o_own,
    hidden_sem,
    small_sem,
    w_sem,
    ring_send,
    ring_recv,
    sib_send,
    sib_recv,
    own_send,
    own_recv,
    q_send_sem,
    q_recv_sem,
    qp_send_sem,
    qp_recv_sem,
    o_send_sem,
    o_recv_sem,
    l_send_sem,
    l_recv_sem,
):
    depth, columns = w_ref.shape
    rows = hidden_vm.shape[1]
    q_rows, q_width = q_ref.shape
    padded = h_blocks.shape[1]
    heads = columns // (2 * HEAD_WIDTH)
    group = q_width // HEAD_WIDTH // heads
    group_width = group * HEAD_WIDTH
    ring = n_roll // 2
    half_ring = ring // 2
    phases = phase_plan(heads)

    me = lax.axis_index("roll")
    seq = lax.axis_index("seq")
    core = me % 2
    chip = me // 2
    along = chip // 2
    side = chip % 2
    place = along * (1 - side) + (ring - 1 - along) * side

    def roll_of(position, which_core):
        position = (position + 2 * ring) % ring
        high = position // half_ring
        where = (1 - high) * (2 * position) + high * (2 * (ring - 1 - position) + 1)
        return 2 * where + which_core

    right = roll_of(place + 1, core)
    left = roll_of(place - 1, core)
    sibling = 2 * chip + 1 - core

    w_copies = [
        pltpu.make_async_copy(w_ref.at[:, pl.ds(h * 128, 128)], w_all.at[me, h], w_sem.at[h])
        for h in range(heads)
    ]
    small_copies = [
        pltpu.make_async_copy(source, target, small_sem.at[n])
        for n, (source, target) in enumerate(
            (
                (q_hbm, q_ref),
                (query_pos_hbm, query_pos_ref),
                (freq_hbm, freq_ref),
                (key_pos_hbm, key_pos_ref),
            )
        )
    ]
    hidden_copy = pltpu.make_async_copy(hidden_ref, hidden_vm, hidden_sem)
    for copy in w_copies + small_copies + [hidden_copy]:
        copy.start()

    barrier = pltpu.get_barrier_semaphore()
    for other in (left, right, sibling):
        pl.semaphore_signal(barrier, inc=1, device_id=(other, seq), device_id_type=MESH)
    for i in range(1, n_seq):
        pl.semaphore_signal(
            barrier, inc=1, device_id=(me, (seq + i) % n_seq), device_id_type=MESH
        )
    pl.semaphore_wait(barrier, 3 + n_seq - 1)

    def some_heads(phase, part):
        first, count = phases[phase]
        if part is None:
            return pl.ds(first, count)
        return pl.ds(first + part * (count // 2), count // 2)

    def origin_of(direction, step, which_core):
        return roll_of(place - step * (1 - 2 * direction), which_core)

    def ring_copy(phase, direction, step, part, arrival=False):
        origin = origin_of(direction, step if arrival else step - 1, core)
        block = w_all.at[origin, some_heads(phase, part)]
        return pltpu.make_async_remote_copy(
            src_ref=block,
            dst_ref=block,
            send_sem=ring_send.at[phase, direction, step - 1],
            recv_sem=ring_recv.at[phase, direction, step - 1],
            device_id=(right if direction == 0 else left, seq),
            device_id_type=MESH,
        )

    def ring_arrival(phase, direction, step, part):
        return ring_copy(phase, direction, step, part, arrival=True)

    def sib_copy(phase, direction, step, part, which_core):
        block = w_all.at[origin_of(direction, step, which_core), some_heads(phase, part)]
        return pltpu.make_async_remote_copy(
            src_ref=block,
            dst_ref=block,
            send_sem=sib_send.at[phase, direction, step - 1],
            recv_sem=sib_recv.at[phase, direction, step - 1],
            device_id=(sibling, seq),
            device_id_type=MESH,
        )

    def sib_own(origin):
        return pltpu.make_async_remote_copy(
            src_ref=w_all.at[origin],
            dst_ref=w_all.at[origin],
            send_sem=own_send,
            recv_sem=own_recv,
            device_id=(sibling, seq),
            device_id_type=MESH,
        )

    def start_phase(phase):
        for direction in range(2):
            ring_copy(phase, direction, 1, None).start()

    def wait_own(phase):
        first, count = phases[phase]
        for h in range(first, first + count):
            w_copies[h].wait()

    wait_own(0)
    start_phase(0)
    for phase in range(1, len(phases)):
        wait_own(phase)
    sib_own(me).start()
    start_phase(1)
    for copy in small_copies:
        copy.wait()

    lane = lax.broadcasted_iota(jnp.int32, (q_rows, 128), 1)
    on_diag = lax.broadcasted_iota(jnp.int32, (q_rows, q_rows), 0) == lax.broadcasted_iota(
        jnp.int32, (q_rows, q_rows), 1
    )
    q_pos_row = query_pos_ref[...].astype(jnp.float32)
    q_pos_col = jnp.sum(
        jnp.where(on_diag, jnp.broadcast_to(q_pos_row, (q_rows, q_rows)), 0.0),
        axis=1,
        keepdims=True,
    )
    qpos_all[seq] = jnp.broadcast_to(q_pos_col, (q_rows, 128))
    freq_row = freq_ref[...]
    q_angle = q_pos_col * freq_row
    q_cos = jnp.cos(q_angle)
    q_sin = jnp.sin(q_angle)
    first_half = lane % HEAD_WIDTH < HEAD_WIDTH // 2
    q_sin = jnp.where(first_half, -q_sin, q_sin)
    scale = HEAD_WIDTH ** -0.5
    for t in range(q_width // 128):
        x = q_ref[:, t * 128 : (t + 1) * 128].astype(jnp.float32)
        swapped = jnp.where(
            first_half,
            pltpu.roll(x, 128 - HEAD_WIDTH // 2, 1),
            pltpu.roll(x, HEAD_WIDTH // 2, 1),
        )
        rotated = (x * q_cos + swapped * q_sin).astype(jnp.bfloat16)
        q_all[seq, :, t * 128 : (t + 1) * 128] = (
            rotated.astype(jnp.float32) * scale
        ).astype(jnp.bfloat16)

    def q_copies(i, origin):
        target = (me, (seq + i) % n_seq)
        return (
            pltpu.make_async_remote_copy(
                src_ref=q_all.at[origin],
                dst_ref=q_all.at[origin],
                send_sem=q_send_sem.at[i],
                recv_sem=q_recv_sem.at[i],
                device_id=target,
                device_id_type=MESH,
            ),
            pltpu.make_async_remote_copy(
                src_ref=qpos_all.at[origin],
                dst_ref=qpos_all.at[origin],
                send_sem=qp_send_sem.at[i],
                recv_sem=qp_recv_sem.at[i],
                device_id=target,
                device_id_type=MESH,
            ),
        )

    for i in range(1, n_seq):
        for copy in q_copies(i, seq):
            copy.start()

    k_pos = key_pos_ref[...].astype(jnp.float32)
    half = HEAD_WIDTH // 2
    pick = lax.broadcasted_iota(jnp.int32, (half, 128), 0) == lax.broadcasted_iota(
        jnp.int32, (half, 128), 1
    )
    freq_col = jnp.sum(
        jnp.where(pick, jnp.broadcast_to(freq_row, (half, 128)), 0.0), axis=1, keepdims=True
    )
    k_angle = freq_col * k_pos
    cos_k[...] = jnp.cos(k_angle)
    sin_k[...] = jnp.sin(k_angle)

    hidden_copy.wait()
    tail = padded - depth // 16 * 16
    for b in range(n_roll):
        if padded > depth:
            h_blocks[b, padded - tail :, :] = jnp.zeros((tail, rows), jnp.bfloat16)
        h_blocks[b, :depth, :] = hidden_vm[b * depth : (b + 1) * depth, :]
    together = 128 // math.gcd(padded, 128)
    for b in range(0, n_roll, together):
        turned = jnp.concatenate(
            [h_blocks[block_of[b + n]] for n in range(together)], axis=0
        ).T
        h_all[:, b * padded : (b + together) * padded] = turned
    if padded > depth:
        for b in range(n_roll):
            w_phase[(b + 1) * padded - tail : (b + 1) * padded, :] = jnp.zeros(
                (tail, w_phase.shape[1]), jnp.bfloat16
            )

    def project(phase):
        first, count = phases[phase]
        for b in range(n_roll):
            for j in range(count):
                w_phase[b * padded : b * padded + depth, j * 128 : (j + 1) * 128] = w_all[
                    b, first + j
                ]
        for j in range(0, count, 2):
            acc[:, (first + j) * 128 : (first + j + 2) * 128] = jnp.dot(
                h_all[...],
                w_phase[:, j * 128 : (j + 2) * 128],
                preferred_element_type=jnp.float32,
            )

    def o_copy(i, h):
        c = pl.ds(pl.multiple_of(h * group_width, group_width), group_width)
        return pltpu.make_async_remote_copy(
            src_ref=o_send.at[i, :, c],
            dst_ref=o_recv.at[i, :, c],
            send_sem=o_send_sem.at[i, h],
            recv_sem=o_recv_sem.at[i, h],
            device_id=(me, (seq + i) % n_seq),
            device_id_type=MESH,
        )

    def l_copy(i):
        return pltpu.make_async_remote_copy(
            src_ref=l_send.at[i],
            dst_ref=l_recv.at[i],
            send_sem=l_send_sem.at[i],
            recv_sem=l_recv_sem.at[i],
            device_id=(me, (seq + i) % n_seq),
            device_id_type=MESH,
        )

    left_lanes = lane < HEAD_WIDTH
    pairs = group // 2

    def attend(i, h, keys, values):
        target = (seq + i) % n_seq
        base = h * group_width
        queries = q_all[target, :, pl.ds(pl.multiple_of(base, group_width), group_width)]
        parts = []
        for j in range(pairs):
            two = queries[:, j * 128 : (j + 1) * 128]
            parts.append(jnp.where(left_lanes, two, jnp.zeros_like(two)))
            parts.append(jnp.where(left_lanes, jnp.zeros_like(two), two))
        stacked = jnp.concatenate(parts, axis=0)
        allowed = k_pos <= qpos_all[target][:, 0:1]
        scores = jnp.dot(stacked, keys, preferred_element_type=jnp.float32)
        scores = scores.reshape(group, q_rows, rows)
        scores = jnp.where(allowed[None], scores, MASKED).reshape(group * q_rows, rows)
        top = jnp.max(scores, axis=1, keepdims=True)
        probs = jnp.exp(scores - top).astype(jnp.bfloat16)
        result = jnp.dot(probs, values, preferred_element_type=jnp.float32)
        total = result[:, 128:]
        normal = result[:, :128] / total
        logs = top + jnp.log(total)
        packed = l_send[i]
        for j in range(pairs):
            even = slice(2 * j * q_rows, (2 * j + 1) * q_rows)
            odd = slice((2 * j + 1) * q_rows, (2 * j + 2) * q_rows)
            tile = jnp.where(left_lanes, normal[even], normal[odd])
            c = pl.ds(pl.multiple_of(base + j * 128, 128), 128)
            if i == 0:
                o_own[:, c] = tile
            else:
                o_send[i, :, c] = tile.astype(jnp.bfloat16)
            packed = jnp.where(lane == h * group + 2 * j, logs[even], packed)
            packed = jnp.where(lane == h * group + 2 * j + 1, logs[odd], packed)
        l_send[i] = packed

    l_send[...] = jnp.zeros_like(l_send)
    lane_k = lax.broadcasted_iota(jnp.int32, (rows, 128), 1)

    def one_head(h):
        both = acc[:, pl.ds(pl.multiple_of(h * 128, 128), 128)]
        turned = both.T
        first = turned[: HEAD_WIDTH // 2]
        second = turned[HEAD_WIDTH // 2 : HEAD_WIDTH]
        cos_keys = cos_k[...]
        sin_keys = sin_k[...]
        key = jnp.concatenate(
            [first * cos_keys - second * sin_keys, second * cos_keys + first * sin_keys], axis=0
        )
        keys = jnp.concatenate([key, key], axis=0).astype(jnp.bfloat16)
        value = jnp.where(lane_k < HEAD_WIDTH, pltpu.roll(both, HEAD_WIDTH, 1), both)
        values = jnp.concatenate([value, jnp.ones_like(value)], axis=1).astype(jnp.bfloat16)
        for i in list(range(1, n_seq)) + [0]:
            attend(i, h, keys, values)
        for i in range(1, n_seq):
            o_copy(i, h).start()

    for phase in range(len(phases)):
        before, before_count = phases[phase - 1] if phase else (0, 0)
        in_loop = min(before_count, half_ring - 1)

        def step_body(step, carry):
            for direction in range(2):
                ring_arrival(phase, direction, step, None).wait_recv()

                @pl.when(step < half_ring - 1)
                def _():
                    ring_copy(phase, direction, step + 1, None).start()

                @pl.when(step == half_ring - 1)
                def _():
                    ring_copy(phase, direction, step + 1, direction).start()

                sib_copy(phase, direction, step, None, core).start()

            if in_loop:

                @pl.when(step <= in_loop)
                def _():
                    one_head(before + step - 1)

            return carry

        lax.fori_loop(1, half_ring, step_body, 0)
        if phase + 2 < len(phases):
            start_phase(phase + 2)
        if phase == 0:
            sib_own(sibling).wait_recv()
            for i in range(1, n_seq):
                for copy in q_copies(i, (seq - i + n_seq) % n_seq):
                    copy.wait_recv()
        for direction in range(2):
            ring_arrival(phase, direction, half_ring, direction).wait_recv()
            sib_copy(phase, direction, half_ring, direction, core).start()
        for left_over in range(in_loop, before_count):
            one_head(before + left_over)

        def sib_step(step, carry):
            for direction in range(2):
                sib_copy(phase, direction, step, None, 1 - core).wait_recv()
            return carry

        lax.fori_loop(1, half_ring, sib_step, 0)
        for direction in range(2):
            sib_copy(phase, direction, half_ring, direction, 1 - core).wait_recv()
        project(phase)

    last, last_count = phases[-1]
    for j in range(last_count):
        one_head(last + j)
    for i in range(1, n_seq):
        l_copy(i).start()

    for i in range(1, n_seq):
        l_copy(i).wait_recv()

        def wait_head(h, carry):
            o_copy(i, h).wait_recv()
            return carry

        lax.fori_loop(0, heads, wait_head, 0)

    logs = [l_send[0]] + [l_recv[i] for i in range(1, n_seq)]
    top = functools.reduce(jnp.maximum, logs)
    shares = [jnp.exp(entry - top) for entry in logs]
    whole = functools.reduce(jnp.add, shares)
    shares = [entry / whole for entry in shares]
    for t in range(q_width // 128):
        c = slice(t * 128, (t + 1) * 128)
        total = None
        for i in range(n_seq):
            share = jnp.where(
                left_lanes, shares[i][:, 2 * t : 2 * t + 1], shares[i][:, 2 * t + 1 : 2 * t + 2]
            )
            part = o_own[:, c] if i == 0 else o_recv[i, :, c].astype(jnp.float32)
            total = share * part if total is None else total + share * part
        out_ref[:, c] = total.astype(jnp.bfloat16)

    for i in range(1, n_seq):
        for copy in q_copies(i, seq):
            copy.wait_send()
        l_copy(i).wait_send()

        def sent_head(h, carry):
            o_copy(i, h).wait_send()
            return carry

        lax.fori_loop(0, heads, sent_head, 0)
    sib_own(me).wait_send()
    for phase in range(len(phases)):

        def sent_step(step, carry):
            for direction in range(2):
                ring_copy(phase, direction, step, None).wait_send()
                sib_copy(phase, direction, step, None, core).wait_send()
            return carry

        lax.fori_loop(1, half_ring, sent_step, 0)
        for direction in range(2):
            ring_copy(phase, direction, half_ring, direction).wait_send()
            sib_copy(phase, direction, half_ring, direction, core).wait_send()


def shards(n_roll, n_seq, hidden, key_value_blocks, block_of, queries, key_pos, query_pos):
    rows, model_width = hidden.shape[1:]
    depth, columns = key_value_blocks.shape
    q_rows, q_width = queries.shape[1:]
    heads = columns // (2 * HEAD_WIDTH)
    half = HEAD_WIDTH // 2
    freq = rope_base ** (-(np.arange(half) * 2.0 / HEAD_WIDTH))
    freq = freq.astype(np.float32)
    vmem = pl.BlockSpec(memory_space=pltpu.VMEM)
    half_ring = n_roll // 4
    phases = len(phase_plan(heads))
    padded = -(-depth // 16) * 16
    anywhere = pl.BlockSpec(memory_space=pl.ANY)
    bf16, f32 = jnp.bfloat16, jnp.float32
    dma = pltpu.SemaphoreType.DMA
    out = pl.pallas_call(
        functools.partial(kernel, n_roll, n_seq),
        out_shape=jax.ShapeDtypeStruct((q_rows, q_width), bf16),
        in_specs=[
            pl.BlockSpec(memory_space=pltpu.SMEM),
            anywhere,
            anywhere,
            anywhere,
            anywhere,
            anywhere,
            anywhere,
        ],
        out_specs=vmem,
        scratch_shapes=[
            pltpu.VMEM((q_rows, q_width), bf16),
            pltpu.VMEM((1, rows), jnp.int32),
            pltpu.VMEM((1, q_rows), jnp.int32),
            pltpu.VMEM((1, 128), f32),
            pltpu.VMEM((n_roll, heads, depth, 128), bf16),
            pltpu.VMEM((model_width, rows), bf16),
            pltpu.VMEM((n_roll, padded, rows), bf16),
            pltpu.VMEM((rows, n_roll * padded), bf16),
            pltpu.VMEM((n_roll * padded, columns // 2), bf16),
            pltpu.VMEM((rows, columns), f32),
            pltpu.VMEM((half, rows), f32),
            pltpu.VMEM((half, rows), f32),
            pltpu.VMEM((n_seq, q_rows, q_width), bf16),
            pltpu.VMEM((n_seq, q_rows, 128), f32),
            pltpu.VMEM((n_seq, q_rows, q_width), bf16),
            pltpu.VMEM((n_seq, q_rows, q_width), bf16),
            pltpu.VMEM((n_seq, q_rows, 128), f32),
            pltpu.VMEM((n_seq, q_rows, 128), f32),
            pltpu.VMEM((q_rows, q_width), f32),
            dma,
            dma((4,)),
            dma((heads,)),
            dma((phases, 2, half_ring)),
            dma((phases, 2, half_ring)),
            dma((phases, 2, half_ring)),
            dma((phases, 2, half_ring)),
            dma,
            dma,
            dma((n_seq,)),
            dma((n_seq,)),
            dma((n_seq,)),
            dma((n_seq,)),
            dma((n_seq, heads)),
            dma((n_seq, heads)),
            dma((n_seq,)),
            dma((n_seq,)),
        ],
        compiler_params=pltpu.CompilerParams(
            collective_id=0, has_side_effects=True, vmem_limit_bytes=60 * 1024 * 1024
        ),
        cost_estimate=pl.CostEstimate(
            flops=2 * rows * model_width * columns,
            bytes_accessed=2 * rows * model_width,
            transcendentals=0,
        ),
    )(
        block_of,
        key_value_blocks,
        hidden[0].T,
        queries[0],
        key_pos,
        query_pos,
        jnp.asarray(np.tile(freq, 128 // half)[None]),
    )
    return out[None]


def solution(mesh):
    return jax.shard_map(
        functools.partial(shards, mesh.shape["roll"], mesh.shape["seq"]),
        mesh=mesh,
        in_specs=(
            P("roll", "seq", None),
            P("roll", None),
            P(),
            P("roll", "seq", None),
            P("roll", "seq"),
            P("roll", "seq"),
        ),
        out_specs=P("roll", "seq", None),
        check_vma=False,
    )
```

```python
import functools
import math

import jax
import jax.numpy as jnp
import numpy as np
from jax import lax
from jax.experimental import pallas as pl
from jax.experimental.pallas import tpu as pltpu
from jax.sharding import PartitionSpec as P

HEAD_WIDTH = 64
MESH = pl.DeviceIdType.MESH
MASKED = -1e30
rope_base = 150000.0


def phase_plan(heads):
    return tuple((first, 2) for first in range(0, heads, 2))


def kernel(
    n_roll,
    n_seq,
    block_of,
    w_ref,
    hidden_ref,
    q_hbm,
    key_pos_hbm,
    query_pos_hbm,
    freq_hbm,
    out_ref,
    q_ref,
    key_pos_ref,
    query_pos_ref,
    freq_ref,
    w_all,
    hidden_vm,
    h_blocks,
    h_all,
    w_phase,
    acc,
    cos_k,
    sin_k,
    q_all,
    qpos_all,
    o_send,
    o_recv,
    l_send,
    l_recv,
    o_own,
    hidden_sem,
    small_sem,
    w_sem,
    ring_send,
    ring_recv,
    sib_send,
    sib_recv,
    own_send,
    own_recv,
    q_send_sem,
    q_recv_sem,
    qp_send_sem,
    qp_recv_sem,
    o_send_sem,
    o_recv_sem,
    l_send_sem,
    l_recv_sem,
):
    depth, columns = w_ref.shape
    rows = hidden_vm.shape[1]
    q_rows, q_width = q_ref.shape
    padded = h_blocks.shape[1]
    heads = columns // (2 * HEAD_WIDTH)
    group = q_width // HEAD_WIDTH // heads
    group_width = group * HEAD_WIDTH
    ring = n_roll // 2
    half_ring = ring // 2
    phases = phase_plan(heads)

    me = lax.axis_index("roll")
    seq = lax.axis_index("seq")
    core = me % 2
    chip = me // 2
    along = chip // 2
    side = chip % 2
    place = along * (1 - side) + (ring - 1 - along) * side

    def roll_of(position, which_core):
        position = (position + 2 * ring) % ring
        high = position // half_ring
        where = (1 - high) * (2 * position) + high * (2 * (ring - 1 - position) + 1)
        return 2 * where + which_core

    right = roll_of(place + 1, core)
    left = roll_of(place - 1, core)
    sibling = 2 * chip + 1 - core

    w_copies = [
        pltpu.make_async_copy(w_ref.at[:, pl.ds(h * 128, 128)], w_all.at[me, h], w_sem.at[h])
        for h in range(heads)
    ]
    small_copies = [
        pltpu.make_async_copy(source, target, small_sem.at[n])
        for n, (source, target) in enumerate(
            (
                (q_hbm, q_ref),
                (query_pos_hbm, query_pos_ref),
                (freq_hbm, freq_ref),
                (key_pos_hbm, key_pos_ref),
            )
        )
    ]
    hidden_copy = pltpu.make_async_copy(hidden_ref, hidden_vm, hidden_sem)
    for copy in w_copies + small_copies + [hidden_copy]:
        copy.start()

    barrier = pltpu.get_barrier_semaphore()
    for other in (left, right, sibling):
        pl.semaphore_signal(barrier, inc=1, device_id=(other, seq), device_id_type=MESH)
    for i in range(1, n_seq):
        pl.semaphore_signal(
            barrier, inc=1, device_id=(me, (seq + i) % n_seq), device_id_type=MESH
        )
    pl.semaphore_wait(barrier, 3 + n_seq - 1)

    def some_heads(phase, part):
        first, count = phases[phase]
        if part is None:
            return pl.ds(first, count)
        return pl.ds(first + part * (count // 2), count // 2)

    def origin_of(direction, step, which_core):
        return roll_of(place - step * (1 - 2 * direction), which_core)

    def ring_copy(phase, direction, step, part, arrival=False):
        origin = origin_of(direction, step if arrival else step - 1, core)
        block = w_all.at[origin, some_heads(phase, part)]
        return pltpu.make_async_remote_copy(
            src_ref=block,
            dst_ref=block,
            send_sem=ring_send.at[phase, direction, step - 1],
            recv_sem=ring_recv.at[phase, direction, step - 1],
            device_id=(right if direction == 0 else left, seq),
            device_id_type=MESH,
        )

    def ring_arrival(phase, direction, step, part):
        return ring_copy(phase, direction, step, part, arrival=True)

    def sib_copy(phase, direction, step, part, which_core):
        block = w_all.at[origin_of(direction, step, which_core), some_heads(phase, part)]
        return pltpu.make_async_remote_copy(
            src_ref=block,
            dst_ref=block,
            send_sem=sib_send.at[phase, direction, step - 1],
            recv_sem=sib_recv.at[phase, direction, step - 1],
            device_id=(sibling, seq),
            device_id_type=MESH,
        )

    def sib_own(origin):
        return pltpu.make_async_remote_copy(
            src_ref=w_all.at[origin],
            dst_ref=w_all.at[origin],
            send_sem=own_send,
            recv_sem=own_recv,
            device_id=(sibling, seq),
            device_id_type=MESH,
        )

    def start_phase(phase):
        for direction in range(2):
            ring_copy(phase, direction, 1, None).start()

    def wait_own(phase):
        first, count = phases[phase]
        for h in range(first, first + count):
            w_copies[h].wait()

    wait_own(0)
    start_phase(0)
    for phase in range(1, len(phases)):
        wait_own(phase)
    sib_own(me).start()
    start_phase(1)
    for copy in small_copies:
        copy.wait()

    lane = lax.broadcasted_iota(jnp.int32, (q_rows, 128), 1)
    on_diag = lax.broadcasted_iota(jnp.int32, (q_rows, q_rows), 0) == lax.broadcasted_iota(
        jnp.int32, (q_rows, q_rows), 1
    )
    q_pos_row = query_pos_ref[...].astype(jnp.float32)
    q_pos_col = jnp.sum(
        jnp.where(on_diag, jnp.broadcast_to(q_pos_row, (q_rows, q_rows)), 0.0),
        axis=1,
        keepdims=True,
    )
    qpos_all[seq] = jnp.broadcast_to(q_pos_col, (q_rows, 128))
    freq_row = freq_ref[...]
    q_angle = q_pos_col * freq_row
    q_cos = jnp.cos(q_angle)
    q_sin = jnp.sin(q_angle)
    first_half = lane % HEAD_WIDTH < HEAD_WIDTH // 2
    q_sin = jnp.where(first_half, -q_sin, q_sin)
    scale = HEAD_WIDTH ** -0.5
    for t in range(q_width // 128):
        x = q_ref[:, t * 128 : (t + 1) * 128].astype(jnp.float32)
        swapped = jnp.where(
            first_half,
            pltpu.roll(x, 128 - HEAD_WIDTH // 2, 1),
            pltpu.roll(x, HEAD_WIDTH // 2, 1),
        )
        rotated = (x * q_cos + swapped * q_sin).astype(jnp.bfloat16)
        q_all[seq, :, t * 128 : (t + 1) * 128] = (
            rotated.astype(jnp.float32) * scale
        ).astype(jnp.bfloat16)

    def q_copies(i, origin):
        target = (me, (seq + i) % n_seq)
        return (
            pltpu.make_async_remote_copy(
                src_ref=q_all.at[origin],
                dst_ref=q_all.at[origin],
                send_sem=q_send_sem.at[i],
                recv_sem=q_recv_sem.at[i],
                device_id=target,
                device_id_type=MESH,
            ),
            pltpu.make_async_remote_copy(
                src_ref=qpos_all.at[origin],
                dst_ref=qpos_all.at[origin],
                send_sem=qp_send_sem.at[i],
                recv_sem=qp_recv_sem.at[i],
                device_id=target,
                device_id_type=MESH,
            ),
        )

    for i in range(1, n_seq):
        for copy in q_copies(i, seq):
            copy.start()

    k_pos = key_pos_ref[...].astype(jnp.float32)
    half = HEAD_WIDTH // 2
    pick = lax.broadcasted_iota(jnp.int32, (half, 128), 0) == lax.broadcasted_iota(
        jnp.int32, (half, 128), 1
    )
    freq_col = jnp.sum(
        jnp.where(pick, jnp.broadcast_to(freq_row, (half, 128)), 0.0), axis=1, keepdims=True
    )
    k_angle = freq_col * k_pos
    tail = padded - depth // 16 * 16
    together = 128 // math.gcd(padded, 128)

    def cut_hidden():
        hidden_copy.wait()
        for b in range(n_roll):
            if padded > depth:
                h_blocks[b, padded - tail :, :] = jnp.zeros((tail, rows), jnp.bfloat16)
                w_phase[(b + 1) * padded - tail : (b + 1) * padded, :] = jnp.zeros(
                    (tail, w_phase.shape[1]), jnp.bfloat16
                )
            h_blocks[b, :depth, :] = hidden_vm[b * depth : (b + 1) * depth, :]

    def turn_hidden(first, count):
        for b in range(first, first + count, together):
            turned = jnp.concatenate(
                [h_blocks[block_of[b + n]] for n in range(together)], axis=0
            ).T
            h_all[:, b * padded : (b + together) * padded] = turned

    def key_angles():
        cos_k[...] = jnp.cos(k_angle)
        sin_k[...] = jnp.sin(k_angle)

    def project(phase):
        if phase == 0:
            sib_own(sibling).wait_recv()

        def sib_step(step, carry):
            for direction in range(2):
                sib_copy(phase, direction, step, None, 1 - core).wait_recv()
            return carry

        lax.fori_loop(1, half_ring, sib_step, 0)
        for direction in range(2):
            sib_copy(phase, direction, half_ring, direction, 1 - core).wait_recv()
        first, count = phases[phase]
        for b in range(n_roll):
            for j in range(count):
                w_phase[b * padded : b * padded + depth, j * 128 : (j + 1) * 128] = w_all[
                    b, first + j
                ]
        for j in range(0, count, 2):
            acc[:, (first + j) * 128 : (first + j + 2) * 128] = jnp.dot(
                h_all[...],
                w_phase[:, j * 128 : (j + 2) * 128],
                preferred_element_type=jnp.float32,
            )

    def o_copy(i, h):
        c = pl.ds(pl.multiple_of(h * group_width, group_width), group_width)
        return pltpu.make_async_remote_copy(
            src_ref=o_send.at[i, :, c],
            dst_ref=o_recv.at[i, :, c],
            send_sem=o_send_sem.at[i, h],
            recv_sem=o_recv_sem.at[i, h],
            device_id=(me, (seq + i) % n_seq),
            device_id_type=MESH,
        )

    def l_copy(i):
        return pltpu.make_async_remote_copy(
            src_ref=l_send.at[i],
            dst_ref=l_recv.at[i],
            send_sem=l_send_sem.at[i],
            recv_sem=l_recv_sem.at[i],
            device_id=(me, (seq + i) % n_seq),
            device_id_type=MESH,
        )

    left_lanes = lane < HEAD_WIDTH
    pairs = group // 2

    def attend(i, h, keys, values):
        target = (seq + i) % n_seq
        base = h * group_width
        queries = q_all[target, :, pl.ds(pl.multiple_of(base, group_width), group_width)]
        parts = []
        for j in range(pairs):
            two = queries[:, j * 128 : (j + 1) * 128]
            parts.append(jnp.where(left_lanes, two, jnp.zeros_like(two)))
            parts.append(jnp.where(left_lanes, jnp.zeros_like(two), two))
        stacked = jnp.concatenate(parts, axis=0)
        allowed = k_pos <= qpos_all[target][:, 0:1]
        scores = jnp.dot(stacked, keys, preferred_element_type=jnp.float32)
        scores = scores.reshape(group, q_rows, rows)
        scores = jnp.where(allowed[None], scores, MASKED).reshape(group * q_rows, rows)
        top = jnp.max(scores, axis=1, keepdims=True)
        probs = jnp.exp(scores - top).astype(jnp.bfloat16)
        result = jnp.dot(probs, values, preferred_element_type=jnp.float32)
        total = result[:, 128:]
        normal = result[:, :128] / total
        logs = top + jnp.log(total)
        packed = l_send[i]
        for j in range(pairs):
            even = slice(2 * j * q_rows, (2 * j + 1) * q_rows)
            odd = slice((2 * j + 1) * q_rows, (2 * j + 2) * q_rows)
            tile = jnp.where(left_lanes, normal[even], normal[odd])
            c = pl.ds(pl.multiple_of(base + j * 128, 128), 128)
            if i == 0:
                o_own[:, c] = tile
            else:
                o_send[i, :, c] = tile.astype(jnp.bfloat16)
            packed = jnp.where(lane == h * group + 2 * j, logs[even], packed)
            packed = jnp.where(lane == h * group + 2 * j + 1, logs[odd], packed)
        l_send[i] = packed

    l_send[...] = jnp.zeros_like(l_send)
    lane_k = lax.broadcasted_iota(jnp.int32, (rows, 128), 1)

    def one_head(h):
        both = acc[:, pl.ds(pl.multiple_of(h * 128, 128), 128)]
        turned = both.T
        first = turned[: HEAD_WIDTH // 2]
        second = turned[HEAD_WIDTH // 2 : HEAD_WIDTH]
        cos_keys = cos_k[...]
        sin_keys = sin_k[...]
        key = jnp.concatenate(
            [first * cos_keys - second * sin_keys, second * cos_keys + first * sin_keys], axis=0
        )
        keys = jnp.concatenate([key, key], axis=0).astype(jnp.bfloat16)
        value = jnp.where(lane_k < HEAD_WIDTH, pltpu.roll(both, HEAD_WIDTH, 1), both)
        values = jnp.concatenate([value, jnp.ones_like(value)], axis=1).astype(jnp.bfloat16)
        for i in list(range(1, n_seq)) + [0]:
            attend(i, h, keys, values)
        for i in range(1, n_seq):
            o_copy(i, h).start()

    def wait_queries():
        for i in range(1, n_seq):
            for copy in q_copies(i, (seq - i + n_seq) % n_seq):
                copy.wait_recv()

    part = n_roll // 2
    work = [
        [
            cut_hidden,
            functools.partial(turn_hidden, 0, part),
            functools.partial(turn_hidden, part, n_roll - part),
            key_angles,
        ]
    ]
    for first, count in phases:
        work.append(
            [functools.partial(project, len(work) - 1)]
            + [functools.partial(one_head, first + j) for j in range(count)]
        )
    work[1].insert(1, wait_queries)

    for phase in range(len(phases)):
        items = list(work[phase])
        for step in range(1, half_ring + 1):
            whole = step < half_ring
            for direction in range(2):
                piece = None if whole else direction
                ring_arrival(phase, direction, step, piece).wait_recv()
                if whole:
                    further = None if step + 1 < half_ring else direction
                    ring_copy(phase, direction, step + 1, further).start()
                sib_copy(phase, direction, step, piece, core).start()
            if step == half_ring - 1 and phase + 2 < len(phases):
                start_phase(phase + 2)
            if items:
                items.pop(0)()
        for item in items:
            item()
    for item in work[-1]:
        item()
    for i in range(1, n_seq):
        l_copy(i).start()

    for i in range(1, n_seq):
        l_copy(i).wait_recv()

        def wait_head(h, carry):
            o_copy(i, h).wait_recv()
            return carry

        lax.fori_loop(0, heads, wait_head, 0)

    logs = [l_send[0]] + [l_recv[i] for i in range(1, n_seq)]
    top = functools.reduce(jnp.maximum, logs)
    shares = [jnp.exp(entry - top) for entry in logs]
    whole = functools.reduce(jnp.add, shares)
    shares = [entry / whole for entry in shares]
    for t in range(q_width // 128):
        c = slice(t * 128, (t + 1) * 128)
        total = None
        for i in range(n_seq):
            share = jnp.where(
                left_lanes, shares[i][:, 2 * t : 2 * t + 1], shares[i][:, 2 * t + 1 : 2 * t + 2]
            )
            part = o_own[:, c] if i == 0 else o_recv[i, :, c].astype(jnp.float32)
            total = share * part if total is None else total + share * part
        out_ref[:, c] = total.astype(jnp.bfloat16)

    for i in range(1, n_seq):
        for copy in q_copies(i, seq):
            copy.wait_send()
        l_copy(i).wait_send()

        def sent_head(h, carry):
            o_copy(i, h).wait_send()
            return carry

        lax.fori_loop(0, heads, sent_head, 0)
    sib_own(me).wait_send()
    for phase in range(len(phases)):

        def sent_step(step, carry):
            for direction in range(2):
                ring_copy(phase, direction, step, None).wait_send()
                sib_copy(phase, direction, step, None, core).wait_send()
            return carry

        lax.fori_loop(1, half_ring, sent_step, 0)
        for direction in range(2):
            ring_copy(phase, direction, half_ring, direction).wait_send()
            sib_copy(phase, direction, half_ring, direction, core).wait_send()


def shards(n_roll, n_seq, hidden, key_value_blocks, block_of, queries, key_pos, query_pos):
    rows, model_width = hidden.shape[1:]
    depth, columns = key_value_blocks.shape
    q_rows, q_width = queries.shape[1:]
    heads = columns // (2 * HEAD_WIDTH)
    half = HEAD_WIDTH // 2
    freq = rope_base ** (-(np.arange(half) * 2.0 / HEAD_WIDTH))
    freq = freq.astype(np.float32)
    vmem = pl.BlockSpec(memory_space=pltpu.VMEM)
    half_ring = n_roll // 4
    phases = len(phase_plan(heads))
    padded = -(-depth // 16) * 16
    anywhere = pl.BlockSpec(memory_space=pl.ANY)
    bf16, f32 = jnp.bfloat16, jnp.float32
    dma = pltpu.SemaphoreType.DMA
    out = pl.pallas_call(
        functools.partial(kernel, n_roll, n_seq),
        out_shape=jax.ShapeDtypeStruct((q_rows, q_width), bf16),
        in_specs=[
            pl.BlockSpec(memory_space=pltpu.SMEM),
            anywhere,
            anywhere,
            anywhere,
            anywhere,
            anywhere,
            anywhere,
        ],
        out_specs=vmem,
        scratch_shapes=[
            pltpu.VMEM((q_rows, q_width), bf16),
            pltpu.VMEM((1, rows), jnp.int32),
            pltpu.VMEM((1, q_rows), jnp.int32),
            pltpu.VMEM((1, 128), f32),
            pltpu.VMEM((n_roll, heads, depth, 128), bf16),
            pltpu.VMEM((model_width, rows), bf16),
            pltpu.VMEM((n_roll, padded, rows), bf16),
            pltpu.VMEM((rows, n_roll * padded), bf16),
            pltpu.VMEM((n_roll * padded, 256), bf16),
            pltpu.VMEM((rows, columns), f32),
            pltpu.VMEM((half, rows), f32),
            pltpu.VMEM((half, rows), f32),
            pltpu.VMEM((n_seq, q_rows, q_width), bf16),
            pltpu.VMEM((n_seq, q_rows, 128), f32),
            pltpu.VMEM((n_seq, q_rows, q_width), bf16),
            pltpu.VMEM((n_seq, q_rows, q_width), bf16),
            pltpu.VMEM((n_seq, q_rows, 128), f32),
            pltpu.VMEM((n_seq, q_rows, 128), f32),
            pltpu.VMEM((q_rows, q_width), f32),
            dma,
            dma((4,)),
            dma((heads,)),
            dma((phases, 2, half_ring)),
            dma((phases, 2, half_ring)),
            dma((phases, 2, half_ring)),
            dma((phases, 2, half_ring)),
            dma,
            dma,
            dma((n_seq,)),
            dma((n_seq,)),
            dma((n_seq,)),
            dma((n_seq,)),
            dma((n_seq, heads)),
            dma((n_seq, heads)),
            dma((n_seq,)),
            dma((n_seq,)),
        ],
        compiler_params=pltpu.CompilerParams(
            collective_id=0, has_side_effects=True, vmem_limit_bytes=60 * 1024 * 1024
        ),
        cost_estimate=pl.CostEstimate(
            flops=2 * rows * model_width * columns,
            bytes_accessed=2 * rows * model_width,
            transcendentals=0,
        ),
    )(
        block_of,
        key_value_blocks,
        hidden[0].T,
        queries[0],
        key_pos,
        query_pos,
        jnp.asarray(np.tile(freq, 128 // half)[None]),
    )
    return out[None]


def solution(mesh):
    return jax.shard_map(
        functools.partial(shards, mesh.shape["roll"], mesh.shape["seq"]),
        mesh=mesh,
        in_specs=(
            P("roll", "seq", None),
            P("roll", None),
            P(),
            P("roll", "seq", None),
            P("roll", "seq"),
            P("roll", "seq"),
        ),
        out_specs=P("roll", "seq", None),
        check_vma=False,
    )
```

```python
import functools
import math

import jax
import jax.numpy as jnp
import numpy as np
from jax import lax
from jax.experimental import pallas as pl
from jax.experimental.pallas import tpu as pltpu
from jax.sharding import PartitionSpec as P

HEAD_WIDTH = 64
MESH = pl.DeviceIdType.MESH
MASKED = -1e30
rope_base = 150000.0


def phase_plan(heads):
    return tuple((first, 2) for first in range(0, heads, 2))


def kernel(
    n_roll,
    n_seq,
    block_of,
    w_ref,
    hidden_ref,
    q_hbm,
    key_pos_hbm,
    query_pos_hbm,
    freq_hbm,
    out_ref,
    q_ref,
    key_pos_ref,
    query_pos_ref,
    freq_ref,
    w_all,
    hidden_vm,
    h_blocks,
    h_all,
    w_phase,
    acc,
    cos_k,
    sin_k,
    q_all,
    qpos_all,
    o_send,
    o_recv,
    l_send,
    l_recv,
    o_own,
    hidden_sem,
    small_sem,
    w_sem,
    ring_send,
    ring_recv,
    sib_send,
    sib_recv,
    own_send,
    own_recv,
    q_send_sem,
    q_recv_sem,
    qp_send_sem,
    qp_recv_sem,
    o_send_sem,
    o_recv_sem,
    l_send_sem,
    l_recv_sem,
):
    depth, columns = w_ref.shape
    rows = hidden_vm.shape[1]
    q_rows, q_width = q_ref.shape
    padded = h_blocks.shape[1]
    heads = columns // (2 * HEAD_WIDTH)
    group = q_width // HEAD_WIDTH // heads
    group_width = group * HEAD_WIDTH
    ring = n_roll // 2
    half_ring = ring // 2
    phases = phase_plan(heads)

    me = lax.axis_index("roll")
    seq = lax.axis_index("seq")
    core = me % 2
    chip = me // 2
    along = chip // 2
    side = chip % 2
    place = along * (1 - side) + (ring - 1 - along) * side

    def roll_of(position, which_core):
        position = (position + 2 * ring) % ring
        high = position // half_ring
        where = (1 - high) * (2 * position) + high * (2 * (ring - 1 - position) + 1)
        return 2 * where + which_core

    right = roll_of(place + 1, core)
    left = roll_of(place - 1, core)
    sibling = 2 * chip + 1 - core

    w_copies = [
        pltpu.make_async_copy(w_ref.at[:, pl.ds(h * 128, 128)], w_all.at[me, h], w_sem.at[h])
        for h in range(heads)
    ]
    small_copies = [
        pltpu.make_async_copy(source, target, small_sem.at[n])
        for n, (source, target) in enumerate(
            (
                (q_hbm, q_ref),
                (query_pos_hbm, query_pos_ref),
                (freq_hbm, freq_ref),
                (key_pos_hbm, key_pos_ref),
            )
        )
    ]
    hidden_copy = pltpu.make_async_copy(hidden_ref, hidden_vm, hidden_sem)
    for copy in w_copies + small_copies + [hidden_copy]:
        copy.start()

    barrier = pltpu.get_barrier_semaphore()
    for other in (left, right, sibling):
        pl.semaphore_signal(barrier, inc=1, device_id=(other, seq), device_id_type=MESH)
    for i in range(1, n_seq):
        pl.semaphore_signal(
            barrier, inc=1, device_id=(me, (seq + i) % n_seq), device_id_type=MESH
        )
    pl.semaphore_wait(barrier, 3 + n_seq - 1)

    def some_heads(phase, part):
        first, count = phases[phase]
        if part is None:
            return pl.ds(first, count)
        return pl.ds(first + part * (count // 2), count // 2)

    def origin_of(direction, step, which_core):
        return roll_of(place - step * (1 - 2 * direction), which_core)

    def ring_copy(phase, direction, step, part, arrival=False):
        origin = origin_of(direction, step if arrival else step - 1, core)
        block = w_all.at[origin, some_heads(phase, part)]
        return pltpu.make_async_remote_copy(
            src_ref=block,
            dst_ref=block,
            send_sem=ring_send.at[phase, direction, step - 1],
            recv_sem=ring_recv.at[phase, direction, step - 1],
            device_id=(right if direction == 0 else left, seq),
            device_id_type=MESH,
        )

    def ring_arrival(phase, direction, step, part):
        return ring_copy(phase, direction, step, part, arrival=True)

    def sib_copy(phase, direction, step, part, which_core):
        block = w_all.at[origin_of(direction, step, which_core), some_heads(phase, part)]
        return pltpu.make_async_remote_copy(
            src_ref=block,
            dst_ref=block,
            send_sem=sib_send.at[phase, direction, step - 1],
            recv_sem=sib_recv.at[phase, direction, step - 1],
            device_id=(sibling, seq),
            device_id_type=MESH,
        )

    def sib_own(origin):
        return pltpu.make_async_remote_copy(
            src_ref=w_all.at[origin],
            dst_ref=w_all.at[origin],
            send_sem=own_send,
            recv_sem=own_recv,
            device_id=(sibling, seq),
            device_id_type=MESH,
        )

    def start_phase(phase):
        for direction in range(2):
            ring_copy(phase, direction, 1, None).start()

    def wait_own(phase):
        first, count = phases[phase]
        for h in range(first, first + count):
            w_copies[h].wait()

    wait_own(0)
    start_phase(0)
    for phase in range(1, len(phases)):
        wait_own(phase)
    sib_own(me).start()
    start_phase(1)
    for copy in small_copies:
        copy.wait()

    lane = lax.broadcasted_iota(jnp.int32, (q_rows, 128), 1)
    on_diag = lax.broadcasted_iota(jnp.int32, (q_rows, q_rows), 0) == lax.broadcasted_iota(
        jnp.int32, (q_rows, q_rows), 1
    )
    q_pos_row = query_pos_ref[...].astype(jnp.float32)
    q_pos_col = jnp.sum(
        jnp.where(on_diag, jnp.broadcast_to(q_pos_row, (q_rows, q_rows)), 0.0),
        axis=1,
        keepdims=True,
    )
    qpos_all[seq] = jnp.broadcast_to(q_pos_col, (q_rows, 128))
    freq_row = freq_ref[...]
    q_angle = q_pos_col * freq_row
    q_cos = jnp.cos(q_angle)
    q_sin = jnp.sin(q_angle)
    first_half = lane % HEAD_WIDTH < HEAD_WIDTH // 2
    q_sin = jnp.where(first_half, -q_sin, q_sin)
    scale = HEAD_WIDTH ** -0.5
    for t in range(q_width // 128):
        x = q_ref[:, t * 128 : (t + 1) * 128].astype(jnp.float32)
        swapped = jnp.where(
            first_half,
            pltpu.roll(x, 128 - HEAD_WIDTH // 2, 1),
            pltpu.roll(x, HEAD_WIDTH // 2, 1),
        )
        rotated = (x * q_cos + swapped * q_sin).astype(jnp.bfloat16)
        q_all[seq, :, t * 128 : (t + 1) * 128] = (
            rotated.astype(jnp.float32) * scale
        ).astype(jnp.bfloat16)

    def q_copies(i, origin):
        target = (me, (seq + i) % n_seq)
        return (
            pltpu.make_async_remote_copy(
                src_ref=q_all.at[origin],
                dst_ref=q_all.at[origin],
                send_sem=q_send_sem.at[i],
                recv_sem=q_recv_sem.at[i],
                device_id=target,
                device_id_type=MESH,
            ),
            pltpu.make_async_remote_copy(
                src_ref=qpos_all.at[origin],
                dst_ref=qpos_all.at[origin],
                send_sem=qp_send_sem.at[i],
                recv_sem=qp_recv_sem.at[i],
                device_id=target,
                device_id_type=MESH,
            ),
        )

    for i in range(1, n_seq):
        for copy in q_copies(i, seq):
            copy.start()

    k_pos = key_pos_ref[...].astype(jnp.float32)
    half = HEAD_WIDTH // 2
    pick = lax.broadcasted_iota(jnp.int32, (half, 128), 0) == lax.broadcasted_iota(
        jnp.int32, (half, 128), 1
    )
    freq_col = jnp.sum(
        jnp.where(pick, jnp.broadcast_to(freq_row, (half, 128)), 0.0), axis=1, keepdims=True
    )
    k_angle = freq_col * k_pos
    tail = padded - depth // 16 * 16
    together = 128 // math.gcd(padded, 128)

    def cut_hidden():
        hidden_copy.wait()
        for b in range(n_roll):
            if padded > depth:
                h_blocks[b, padded - tail :, :] = jnp.zeros((tail, rows), jnp.bfloat16)
                w_phase[(b + 1) * padded - tail : (b + 1) * padded, :] = jnp.zeros(
                    (tail, w_phase.shape[1]), jnp.bfloat16
                )
            h_blocks[b, :depth, :] = hidden_vm[b * depth : (b + 1) * depth, :]

    def turn_hidden(first, count):
        for b in range(first, first + count, together):
            turned = jnp.concatenate(
                [h_blocks[block_of[b + n]] for n in range(together)], axis=0
            ).T
            h_all[:, b * padded : (b + together) * padded] = turned

    def key_angles():
        cos_k[...] = jnp.cos(k_angle)
        sin_k[...] = jnp.sin(k_angle)

    def project(phase):
        if phase == 0:
            sib_own(sibling).wait_recv()

        def sib_step(step, carry):
            for direction in range(2):
                sib_copy(phase, direction, step, None, 1 - core).wait_recv()
            return carry

        lax.fori_loop(1, half_ring, sib_step, 0)
        for direction in range(2):
            sib_copy(phase, direction, half_ring, direction, 1 - core).wait_recv()
        first, count = phases[phase]
        for b in range(n_roll):
            for j in range(count):
                w_phase[b * padded : b * padded + depth, j * 128 : (j + 1) * 128] = w_all[
                    b, first + j
                ]
        for j in range(0, count, 2):
            acc[:, (first + j) * 128 : (first + j + 2) * 128] = jnp.dot(
                h_all[...],
                w_phase[:, j * 128 : (j + 2) * 128],
                preferred_element_type=jnp.float32,
            )

    def o_copy(i, h):
        c = pl.ds(pl.multiple_of(h * group_width, group_width), group_width)
        return pltpu.make_async_remote_copy(
            src_ref=o_send.at[i, :, c],
            dst_ref=o_recv.at[i, :, c],
            send_sem=o_send_sem.at[i, h],
            recv_sem=o_recv_sem.at[i, h],
            device_id=(me, (seq + i) % n_seq),
            device_id_type=MESH,
        )

    def l_copy(i):
        return pltpu.make_async_remote_copy(
            src_ref=l_send.at[i],
            dst_ref=l_recv.at[i],
            send_sem=l_send_sem.at[i],
            recv_sem=l_recv_sem.at[i],
            device_id=(me, (seq + i) % n_seq),
            device_id_type=MESH,
        )

    left_lanes = lane < HEAD_WIDTH
    pairs = group // 2

    def attend(i, h, keys, values):
        target = (seq + i) % n_seq
        base = h * group_width
        queries = q_all[target, :, pl.ds(pl.multiple_of(base, group_width), group_width)]
        parts = []
        for j in range(pairs):
            two = queries[:, j * 128 : (j + 1) * 128]
            parts.append(jnp.where(left_lanes, two, jnp.zeros_like(two)))
            parts.append(jnp.where(left_lanes, jnp.zeros_like(two), two))
        stacked = jnp.concatenate(parts, axis=0)
        allowed = k_pos <= qpos_all[target][:, 0:1]
        scores = jnp.dot(stacked, keys, preferred_element_type=jnp.float32)
        scores = scores.reshape(group, q_rows, rows)
        scores = jnp.where(allowed[None], scores, MASKED).reshape(group * q_rows, rows)
        top = jnp.max(scores, axis=1, keepdims=True)
        probs = jnp.exp(scores - top).astype(jnp.bfloat16)
        result = jnp.dot(probs, values, preferred_element_type=jnp.float32)
        total = result[:, 128:]
        normal = result[:, :128] / total
        logs = top + jnp.log(total)
        packed = l_send[i]
        for j in range(pairs):
            even = slice(2 * j * q_rows, (2 * j + 1) * q_rows)
            odd = slice((2 * j + 1) * q_rows, (2 * j + 2) * q_rows)
            tile = jnp.where(left_lanes, normal[even], normal[odd])
            c = pl.ds(pl.multiple_of(base + j * 128, 128), 128)
            if i == 0:
                o_own[:, c] = tile
            else:
                o_send[i, :, c] = tile.astype(jnp.bfloat16)
            packed = jnp.where(lane == h * group + 2 * j, logs[even], packed)
            packed = jnp.where(lane == h * group + 2 * j + 1, logs[odd], packed)
        l_send[i] = packed

    l_send[...] = jnp.zeros_like(l_send)
    lane_k = lax.broadcasted_iota(jnp.int32, (rows, 128), 1)

    def one_head(h):
        both = acc[:, pl.ds(pl.multiple_of(h * 128, 128), 128)]
        turned = both.T
        first = turned[: HEAD_WIDTH // 2]
        second = turned[HEAD_WIDTH // 2 : HEAD_WIDTH]
        cos_keys = cos_k[...]
        sin_keys = sin_k[...]
        key = jnp.concatenate(
            [first * cos_keys - second * sin_keys, second * cos_keys + first * sin_keys], axis=0
        )
        keys = jnp.concatenate([key, key], axis=0).astype(jnp.bfloat16)
        value = jnp.where(lane_k < HEAD_WIDTH, pltpu.roll(both, HEAD_WIDTH, 1), both)
        values = jnp.concatenate([value, jnp.ones_like(value)], axis=1).astype(jnp.bfloat16)
        for i in list(range(1, n_seq)) + [0]:
            attend(i, h, keys, values)
        for i in range(1, n_seq):
            o_copy(i, h).start()

    def wait_queries():
        for i in range(1, n_seq):
            for copy in q_copies(i, (seq - i + n_seq) % n_seq):
                copy.wait_recv()

    part = n_roll // 2
    count = len(phases)
    work = [
        cut_hidden,
        functools.partial(turn_hidden, 0, part),
        functools.partial(turn_hidden, part, n_roll - part),
        key_angles,
    ]
    later = [wait_queries]
    for phase in range(count):
        later.append(functools.partial(project, phase))
        first, many = phases[phase]
        later += [functools.partial(one_head, first + j) for j in range(many)]

    for tick in range(1, half_ring + count):
        for phase in range(count):
            step = tick - phase
            if not 1 <= step <= half_ring:
                continue
            whole = step < half_ring
            for direction in range(2):
                piece = None if whole else direction
                ring_arrival(phase, direction, step, piece).wait_recv()
                if whole:
                    further = None if step + 1 < half_ring else direction
                    ring_copy(phase, direction, step + 1, further).start()
                sib_copy(phase, direction, step, piece, core).start()
        if 2 <= tick + 1 < count:
            start_phase(tick + 1)
        if work:
            work.pop(0)()
        elif tick > half_ring:
            for _ in range(2):
                later.pop(0)()
    for item in later:
        item()
    for i in range(1, n_seq):
        l_copy(i).start()

    for i in range(1, n_seq):
        l_copy(i).wait_recv()

        def wait_head(h, carry):
            o_copy(i, h).wait_recv()
            return carry

        lax.fori_loop(0, heads, wait_head, 0)

    logs = [l_send[0]] + [l_recv[i] for i in range(1, n_seq)]
    top = functools.reduce(jnp.maximum, logs)
    shares = [jnp.exp(entry - top) for entry in logs]
    whole = functools.reduce(jnp.add, shares)
    shares = [entry / whole for entry in shares]
    for t in range(q_width // 128):
        c = slice(t * 128, (t + 1) * 128)
        total = None
        for i in range(n_seq):
            share = jnp.where(
                left_lanes, shares[i][:, 2 * t : 2 * t + 1], shares[i][:, 2 * t + 1 : 2 * t + 2]
            )
            part = o_own[:, c] if i == 0 else o_recv[i, :, c].astype(jnp.float32)
            total = share * part if total is None else total + share * part
        out_ref[:, c] = total.astype(jnp.bfloat16)

    for i in range(1, n_seq):
        for copy in q_copies(i, seq):
            copy.wait_send()
        l_copy(i).wait_send()

        def sent_head(h, carry):
            o_copy(i, h).wait_send()
            return carry

        lax.fori_loop(0, heads, sent_head, 0)
    sib_own(me).wait_send()
    for phase in range(len(phases)):

        def sent_step(step, carry):
            for direction in range(2):
                ring_copy(phase, direction, step, None).wait_send()
                sib_copy(phase, direction, step, None, core).wait_send()
            return carry

        lax.fori_loop(1, half_ring, sent_step, 0)
        for direction in range(2):
            ring_copy(phase, direction, half_ring, direction).wait_send()
            sib_copy(phase, direction, half_ring, direction, core).wait_send()


def shards(n_roll, n_seq, hidden, key_value_blocks, block_of, queries, key_pos, query_pos):
    rows, model_width = hidden.shape[1:]
    depth, columns = key_value_blocks.shape
    q_rows, q_width = queries.shape[1:]
    heads = columns // (2 * HEAD_WIDTH)
    half = HEAD_WIDTH // 2
    freq = rope_base ** (-(np.arange(half) * 2.0 / HEAD_WIDTH))
    freq = freq.astype(np.float32)
    vmem = pl.BlockSpec(memory_space=pltpu.VMEM)
    half_ring = n_roll // 4
    phases = len(phase_plan(heads))
    padded = -(-depth // 16) * 16
    anywhere = pl.BlockSpec(memory_space=pl.ANY)
    bf16, f32 = jnp.bfloat16, jnp.float32
    dma = pltpu.SemaphoreType.DMA
    out = pl.pallas_call(
        functools.partial(kernel, n_roll, n_seq),
        out_shape=jax.ShapeDtypeStruct((q_rows, q_width), bf16),
        in_specs=[
            pl.BlockSpec(memory_space=pltpu.SMEM),
            anywhere,
            anywhere,
            anywhere,
            anywhere,
            anywhere,
            anywhere,
        ],
        out_specs=vmem,
        scratch_shapes=[
            pltpu.VMEM((q_rows, q_width), bf16),
            pltpu.VMEM((1, rows), jnp.int32),
            pltpu.VMEM((1, q_rows), jnp.int32),
            pltpu.VMEM((1, 128), f32),
            pltpu.VMEM((n_roll, heads, depth, 128), bf16),
            pltpu.VMEM((model_width, rows), bf16),
            pltpu.VMEM((n_roll, padded, rows), bf16),
            pltpu.VMEM((rows, n_roll * padded), bf16),
            pltpu.VMEM((n_roll * padded, 256), bf16),
            pltpu.VMEM((rows, columns), f32),
            pltpu.VMEM((half, rows), f32),
            pltpu.VMEM((half, rows), f32),
            pltpu.VMEM((n_seq, q_rows, q_width), bf16),
            pltpu.VMEM((n_seq, q_rows, 128), f32),
            pltpu.VMEM((n_seq, q_rows, q_width), bf16),
            pltpu.VMEM((n_seq, q_rows, q_width), bf16),
            pltpu.VMEM((n_seq, q_rows, 128), f32),
            pltpu.VMEM((n_seq, q_rows, 128), f32),
            pltpu.VMEM((q_rows, q_width), f32),
            dma,
            dma((4,)),
            dma((heads,)),
            dma((phases, 2, half_ring)),
            dma((phases, 2, half_ring)),
            dma((phases, 2, half_ring)),
            dma((phases, 2, half_ring)),
            dma,
            dma,
            dma((n_seq,)),
            dma((n_seq,)),
            dma((n_seq,)),
            dma((n_seq,)),
            dma((n_seq, heads)),
            dma((n_seq, heads)),
            dma((n_seq,)),
            dma((n_seq,)),
        ],
        compiler_params=pltpu.CompilerParams(
            collective_id=0, has_side_effects=True, vmem_limit_bytes=60 * 1024 * 1024
        ),
        cost_estimate=pl.CostEstimate(
            flops=2 * rows * model_width * columns,
            bytes_accessed=2 * rows * model_width,
            transcendentals=0,
        ),
    )(
        block_of,
        key_value_blocks,
        hidden[0].T,
        queries[0],
        key_pos,
        query_pos,
        jnp.asarray(np.tile(freq, 128 // half)[None]),
    )
    return out[None]


def solution(mesh):
    return jax.shard_map(
        functools.partial(shards, mesh.shape["roll"], mesh.shape["seq"]),
        mesh=mesh,
        in_specs=(
            P("roll", "seq", None),
            P("roll", None),
            P(),
            P("roll", "seq", None),
            P("roll", "seq"),
            P("roll", "seq"),
        ),
        out_specs=P("roll", "seq", None),
        check_vma=False,
    )
```
